32 devices in a mesh: dp: 2 (over x), seq: 16 (over z, y, core).
Axes of the slice: x: 2, y: 2, z: 4, core: 2. Of those that a mesh axis runs over, the one named last changes fastest.
Arguments:
- inputs: float32 [2, 2048, 2048], P('dp', 'seq'), may hold values from -6 to 6
- cotangent: float32 [2, 2048, 2048], P('dp', 'seq'), may hold values from -6 to 6
- block_mix: float32 [128, 128], replicated, may hold values from -0.5 to 0.5
- twist_hi: float32 [2, 2, 2048], replicated, may hold values from -3 to 3
- twist_lo: float32 [2, 2, 2048], replicated, may hold values from -3 to 3
- gain: float32 [2048], replicated, may hold values from 0.5 to 1.5
- gate_up: float32 [128, 2, 16, 256], P('seq'), may hold values from -0.5 to 0.5
- down: float32 [256, 16, 128], P('seq'), may hold values from -0.375 to 0.375
Outputs:
- grad_inputs: float32 [2, 2048, 2048], P('dp', 'seq')
- grad_gate_up: float32 [128, 2, 16, 256], P('seq')
- grad_down: float32 [256, 16, 128], P('seq')
- grad_block_mix: float32 [128, 128], replicated
- grad_twist_hi: float32 [2, 2, 2048], replicated
- grad_twist_lo: float32 [2, 2, 2048], replicated
- grad_gain: float32 [2048], replicated
The draws below stay inside these ranges and needn't reach their ends.
All inputs are finite; a program needn't handle non-finite values.
Results may differ from the reference program's by a relative error of at most 0.00022.
Values sent between devices are 32-bit elements; how exact they have to be, the bound alone decides.
A program may use at most 64 MiB of HBM per device.

```python
import math
import jax
import jax.numpy as jnp
from jax import lax

D = 2048
NB = 16
BLK = 128
TOK_DEV = 128
SHARDS = 16
SEQ_LEN = 2048
SEQS = 2
TOTAL = 4096
DB = 128
FB = 256


def steps_of(key, dims, pieces, least, high):
    factor_of = 1.0
    for dim, shards_of in pieces:
        steps = jax.random.uniform(jax.random.fold_in(jax.random.fold_in(key, 6), dim), (shards_of,), jnp.float32, least / len(pieces), high / len(pieces))
        factor_of = factor_of * jnp.repeat(jnp.exp(steps), dims[dim] // shards_of).reshape((-1,) + (1,) * (len(dims) - 1 - dim))
    return factor_of


def gaussian(own_key, shape, width, limit, split=(), kind=jnp.bfloat16):
    array = jax.random.normal(own_key, shape, jnp.float32) * width
    if len(split) > 0:
        array = steps_of(own_key, shape, split, -0.22, 0.18) * array
    return jnp.clip(array, min=-limit, max=limit).astype(kind)


def setup_inputs(seed: int = 0) -> dict:
    seeds = jax.random.split(jax.random.key(seed), 9)
    return {
        "inputs": gaussian(seeds[0], (SEQS, SEQ_LEN, D), 1.0, 6.0, ((0, 2), (1, 16)), jnp.float32),
        "cotangent": gaussian(seeds[1], (SEQS, SEQ_LEN, D), 1.0, 6.0, ((0, 2), (1, 16)), jnp.float32),
        "block_mix": gaussian(seeds[2], (BLK, BLK), BLK ** -0.5, 0.5, (), jnp.float32),
        "twist_hi": gaussian(seeds[3], (2, 2, D), 0.7, 3.0, (), jnp.float32),
        "twist_lo": gaussian(seeds[4], (2, 2, D), 0.7, 3.0, (), jnp.float32),
        "gain": jnp.clip(1.0 + 0.1 * jax.random.normal(seeds[5], (D,), jnp.float32), 0.5, 1.5),
        "gate_up": gaussian(seeds[6], (DB, 2, NB, FB), DB ** -0.5, 0.5, ((0, 16),), jnp.float32),
        "down": gaussian(seeds[7], (FB, NB, DB), FB ** -0.5, 0.375, ((0, 16),), jnp.float32),
    }


HIGH = lax.Precision.HIGHEST
EPS = 1e-05

def section(field, coeff, distance):
    blocks = field.reshape(SHARDS, TOK_DEV, D)
    index = jnp.arange(SHARDS, dtype=jnp.int32)
    side = index // distance % 2
    partner = index + distance - 2 * distance * side
    own = coeff[side]
    result = own[:, 0][:, None, :] * blocks + own[:, 1][:, None, :] * blocks[partner]
    return result.reshape(SEQ_LEN, D)

def forward(seq_in, block_mix, twist_hi, twist_lo, gain, gate_up, down):
    xb = seq_in.reshape(SEQ_LEN // BLK, BLK, D)
    mixed = jnp.einsum('ij,kjd->kid', block_mix, xb, precision=HIGH).reshape(SEQ_LEN, D)
    first = section(mixed, twist_hi, SHARDS // 2)
    second = section(first, twist_lo, 1)
    resid = seq_in + second
    scale = lax.rsqrt(lax.optimization_barrier(jnp.mean(resid * resid, axis=-1, keepdims=True)) + EPS)
    normed = (resid * scale * gain).reshape(SEQ_LEN, NB, DB)
    gate_val = jnp.einsum('tnd,dnf->tnf', normed, gate_up[:, 0], precision=HIGH)
    up_val = jnp.einsum('tnd,dnf->tnf', normed, gate_up[:, 1], precision=HIGH)
    hidden = jax.nn.silu(gate_val) * up_val
    projected = jnp.einsum('tnf,fnd->tnd', hidden, down, precision=HIGH).reshape(SEQ_LEN, D)
    return resid + projected

def reference(inputs, cotangent, block_mix, twist_hi, twist_lo, gain, gate_up, down):
    params = (block_mix, twist_hi, twist_lo, gain, gate_up, down)

    def one_sequence(carry, pair):
        seq_in, seq_cot = pair
        _, pull = jax.vjp(forward, seq_in, *params)
        grads = pull(seq_cot)
        carry = tuple((c + g for c, g in zip(carry, grads[1:])))
        return (carry, grads[0])
    start = tuple((jnp.zeros(p.shape, jnp.float32) for p in params))
    totals, grad_inputs = lax.scan(one_sequence, start, (inputs, cotangent))
    factor = 1.0 / math.sqrt(TOTAL)
    g_block, g_hi, g_lo, g_gain, g_gu, g_down = [t * factor for t in totals]
    return (grad_inputs, g_gu, g_down, g_block, g_hi, g_lo, g_gain)
```

```python
import functools
import math

import jax
import jax.numpy as jnp
from jax import lax
from jax.experimental import pallas as pl
from jax.experimental.pallas import tpu as pltpu
from jax.sharding import PartitionSpec as P

NB = 16
BLK = 128
DB = 128
FB = 256
EPS = 1e-05
SMALL = 16
F32 = jnp.float32
BF16 = jnp.bfloat16
NN = (((1,), (0,)), ((), ()))
NT = (((1,), (1,)), ((), ()))
TN = (((0,), (0,)), ((), ()))
ORDER = (8, 4, 9, 12, 1, 13, 10, 5, 14, 2, 11, 6, 15, 3, 7)


def xor(a, b, bits):
    total = a + b
    for bit in range(bits):
        total = total - 2 * (1 << bit) * ((a // (1 << bit)) % 2) * ((b // (1 << bit)) % 2)
    return total


def split(value):
    high = value.astype(BF16)
    return high, (value - high.astype(F32)).astype(BF16)


def dot(a, b, dims):
    return lax.dot_general(a, b, dims, preferred_element_type=F32)


def left(value, axis):
    high, low = split(value)
    return jnp.concatenate([high, low, high], axis=axis)


def right(value, axis):
    high, low = split(value)
    return jnp.concatenate([high, high, low], axis=axis)


def row_sums(value):
    high, low = split(value)
    ones = jnp.ones((8, 2 * value.shape[1]), BF16)
    return dot(ones, jnp.concatenate([high, low], axis=1), NT)[0:1]


def as_columns(row):
    return jnp.broadcast_to(row, (DB, row.shape[1])).T


def arrived(ref, sem):
    pltpu.make_async_copy(ref, ref, sem).wait()


def kernel(
    dps, count, factor,
    x_hbm, g_hbm, gu_hbm, dn_hbm, bm_ref, th_ref, tl_ref, gain_ref,
    out_x, out_gu, out_dn, out_small,
    xb, gb, mixed, first, resid, scb, wsc, gseq,
    gu_in, dn_in, gu_f32, dn_f32, gu_k, gu_n, dn_n,
    gu_rep, dn_rep, gu_out, dn_out, sm_rep, sm_tot, bm_in, pack,
    ss_buf, in_buf, rows_ref,
    x_s, x_r, g_s, g_r, gu_s, gu_r, dn_s, dn_r, ss_s, ss_r, in_s, in_r,
    o_s, o_r, gr_s, gr_r, dr_s, dr_r, go_s, go_r, do_s, do_r, sr_s, sr_r,
    bm_s, bm_r, pk_s, pk_r,
):
    groups = count // NB
    bits = count.bit_length() - 1
    reps = dps * groups
    rows, drows = DB // count, FB // count
    me = lax.axis_index("seq")
    dp = lax.axis_index("dp")
    rank = me % 2 + me // (2 * groups) * 2
    group = me // 2 % groups
    rep = dp * groups + group

    def seq_of(rk, grp):
        return rk % 2 + grp * 2 + rk // 2 * 2 * groups

    def peer(k):
        return seq_of(xor(rank, k, 4), group)

    def send(src, dst, ssem, rsem, to_dp, to_seq):
        copy = pltpu.make_async_remote_copy(
            src_ref=src, dst_ref=dst, send_sem=ssem, recv_sem=rsem,
            device_id=(to_dp, to_seq), device_id_type=pl.DeviceIdType.MESH,
        )
        copy.start()
        return copy

    def cols(ref, rk):
        return ref.at[:, pl.ds(pl.multiple_of(rk * DB, DB), DB)]

    replicas = []
    for step in range(1, reps):
        other = (rep + step) % reps
        replicas.append((step, other, other // groups, seq_of(rank, other % groups)))

    barrier = pltpu.get_barrier_semaphore()
    met = 0
    for k in range(1, count):
        pl.semaphore_signal(
            barrier, inc=1, device_id=(dp, xor(me, k, bits)), device_id_type=pl.DeviceIdType.MESH
        )
        met += 1
    for step in range(1, dps):
        for grp in range(groups):
            pl.semaphore_signal(
                barrier, inc=1, device_id=((dp + step) % dps, seq_of(rank, grp)),
                device_id_type=pl.DeviceIdType.MESH,
            )
            met += 1
    pl.semaphore_wait(barrier, met)

    sent = []
    local = [
        pltpu.make_async_copy(cols(x_hbm, rank), xb.at[0], x_r.at[0]),
        pltpu.make_async_copy(cols(g_hbm, rank), gb.at[0], g_r.at[0]),
        pltpu.make_async_copy(gu_hbm.at[rank], gu_in.at[me], gu_r.at[0]),
        pltpu.make_async_copy(dn_hbm.at[rank], dn_in.at[me], dn_r.at[0]),
    ]
    for copy in local:
        copy.start()
    for k in ORDER:
        sent.append(send(cols(x_hbm, xor(rank, k, 4)), xb.at[k], x_s.at[k], x_r.at[k], dp, peer(k)))
    for j in range(1, count):
        k = ORDER[j - 1] if count == NB else j
        to = xor(me, k, bits)
        block = to % 2 + to // (2 * groups) * 2
        sent.append(send(gu_hbm.at[block], gu_in.at[me], gu_s.at[k], gu_r.at[k], dp, to))
        sent.append(send(dn_hbm.at[block], dn_in.at[me], dn_s.at[k], dn_r.at[k], dp, to))

    mix_left = left(bm_ref[...], 1)
    back_left = left(bm_ref[...].T, 1)

    def mix(k, _):
        arrived(xb.at[k], x_r.at[k])
        mixed[k] = dot(mix_left, right(xb[k], 0), NN)
        return 0

    lax.fori_loop(0, NB // 2, mix, 0)
    for k in ORDER:
        sent.append(send(cols(g_hbm, xor(rank, k, 4)), gb.at[k], g_s.at[k], g_r.at[k], dp, peer(k)))
    lax.fori_loop(NB // 2, NB, mix, 0)

    lanes = pl.ds(pl.multiple_of(rank * DB, DB), DB)
    side_hi, side_lo = rank // 8, rank % 2

    def coefficients(ref, side):
        out = []
        for j in range(2):
            pair = ref[side + j - 2 * side * j, :, lanes]
            out.append((pair[0:1], pair[1:2]))
        return out

    hi = coefficients(th_ref, side_hi)
    lo = coefficients(tl_ref, side_lo)
    gain = gain_ref[:, lanes]

    def forward(i, _):
        ks = [2 * i, 2 * i + 1, 2 * i + 8, 2 * i + 9]
        mx = [mixed[k] for k in ks]
        fs = []
        for n in range(4):
            c = hi[n // 2]
            fs.append(c[0] * mx[n] + c[1] * mx[(n + 2) % 4])
            first[ks[n]] = fs[n]
        for n in range(4):
            c = lo[n % 2]
            r = xb[ks[n]] + (c[0] * fs[n] + c[1] * fs[n + 1 - 2 * (n % 2)])
            resid[ks[n]] = r
            ss_buf[0, pl.ds(xor(rank, ks[n], 4), 1), :] = row_sums(r * r)
        return 0

    lax.fori_loop(0, 4, forward, 0)
    for k in ORDER:
        sent.append(send(ss_buf.at[0], ss_buf.at[k], ss_s.at[k], ss_r.at[k], dp, peer(k)))

    for k in range(count):
        owner = xor(me, k, bits)
        arrived(gu_in.at[owner], gu_r.at[k])
        arrived(dn_in.at[owner], dn_r.at[k])
    for s in range(count):
        gu_f32[s * rows : (s + 1) * rows, :] = gu_in[s]
        dn_f32[s * drows : (s + 1) * drows, :] = dn_in[s]
    gu_k[...] = right(gu_f32[...], 0)
    gu_n[...] = right(gu_f32[...], 1)
    dn_n[...] = right(dn_f32[...], 1)
    gu_rep[rep] = jnp.zeros((DB, 2 * FB), F32)
    dn_rep[rep] = jnp.zeros((DB, FB), F32)

    for k in range(1, NB):
        arrived(ss_buf.at[k], ss_r.at[k])
    total = ss_buf[0]
    for k in range(1, NB):
        total = total + ss_buf[k]
    width = NB * DB
    rows_ref[...] = lax.rsqrt(total * (1.0 / width) + EPS)

    def mlp(i, gain_sum):
        scales, resids, cots = [], [], []
        for j in range(2):
            k = 2 * i + j
            arrived(gb.at[k], g_r.at[k])
            sc = as_columns(rows_ref[pl.ds(xor(rank, k, 4), 1), :])
            scb[k] = sc
            scales.append(sc)
            resids.append(resid[k])
            cots.append(gb[k])
        scale = jnp.concatenate(scales, axis=0)
        res = jnp.concatenate(resids, axis=0)
        cot = jnp.concatenate(cots, axis=0)
        unit = res * scale
        nh, nl = split(unit * gain)
        gh, gl = split(cot)
        gu = dot(jnp.concatenate([nh, nl, nh], axis=1), gu_k[...], NN)
        gate, up = gu[:, :FB], gu[:, FB:]
        sig = 1.0 / (1.0 + jnp.exp(-gate))
        act = gate * sig
        grad_hidden = dot(jnp.concatenate([gh, gl, gh], axis=1), dn_n[...], NT)
        hidden = right(act * up, 0)
        grad_gate = grad_hidden * up * sig * (1.0 + gate * (1.0 - sig))
        both_h, both_l = split(jnp.concatenate([grad_gate, grad_hidden * act], axis=1))
        grad_normed = dot(jnp.concatenate([both_h, both_l, both_h], axis=1), gu_n[...], NT)
        gu_rep[rep] += dot(
            jnp.concatenate([nh, nl, nh], axis=0),
            jnp.concatenate([both_h, both_h, both_l], axis=0), TN,
        )
        dn_rep[rep] += dot(jnp.concatenate([gh, gl, gh], axis=0), hidden, TN)
        weighted = grad_normed * gain
        prod = weighted * res
        ws = weighted * scale
        for j in range(2):
            k = 2 * i + j
            wsc[k] = ws[j * BLK : (j + 1) * BLK]
            in_buf[0, pl.ds(xor(rank, k, 4), 1), :] = row_sums(prod[j * BLK : (j + 1) * BLK])
        return gain_sum + jnp.sum(grad_normed * unit, axis=0, keepdims=True)

    gain_sum = lax.fori_loop(0, NB // 2, mlp, jnp.zeros((1, DB), F32))

    for k in ORDER:
        sent.append(send(in_buf.at[0], in_buf.at[k], in_s.at[k], in_r.at[k], dp, peer(k)))
    for step, other, to_dp, to_seq in replicas:
        sent.append(send(gu_rep.at[rep], gu_rep.at[rep], gr_s.at[step], gr_r.at[step], to_dp, to_seq))
        sent.append(send(dn_rep.at[rep], dn_rep.at[rep], dr_s.at[step], dr_r.at[step], to_dp, to_seq))

    for k in range(1, NB):
        arrived(in_buf.at[k], in_r.at[k])
    total = in_buf[0]
    for k in range(1, NB):
        total = total + in_buf[k]
    rows_ref[...] = total * (1.0 / width)

    sm_rep[rep] = jnp.zeros((BLK + SMALL, DB), F32)

    def backward(i, carry):
        q = 3 - i
        ks = [2 * q, 2 * q + 1, 2 * q + 8, 2 * q + 9]
        t_hi, t_lo = list(carry[:4]), list(carry[4:])
        gr = []
        for k in ks:
            inner = as_columns(rows_ref[pl.ds(xor(rank, k, 4), 1), :])
            sc = scb[k]
            gr.append(gb[k] + wsc[k] - resid[k] * sc * sc * sc * inner)
        fs = [first[k] for k in ks]
        mx = [mixed[k] for k in ks]
        gf = []
        for n in range(4):
            j, m = n % 2, n + 1 - 2 * (n % 2)
            gf.append(lo[j][0] * gr[n] + lo[1 - j][1] * gr[m])
            t_lo[2 * j] += jnp.sum(gr[n] * fs[n], axis=0, keepdims=True)
            t_lo[2 * j + 1] += jnp.sum(gr[n] * fs[m], axis=0, keepdims=True)
        for n in range(4):
            j, m = n // 2, (n + 2) % 4
            gm = hi[j][0] * gf[n] + hi[1 - j][1] * gf[m]
            t_hi[2 * j] += jnp.sum(gf[n] * mx[n], axis=0, keepdims=True)
            t_hi[2 * j + 1] += jnp.sum(gf[n] * mx[m], axis=0, keepdims=True)
            mh, ml = split(gm)
            gseq[ks[n]] = dot(back_left, jnp.concatenate([mh, mh, ml], axis=0), NN) + gr[n]
            k = ks[n]

            @pl.when(k != 0)
            def _():
                send(gseq.at[k], cols(out_x, rank), o_s.at[k], o_r.at[k], dp, peer(k))

            sm_rep[rep, :BLK, :] += dot(jnp.concatenate([mh, ml, mh], axis=1), right(xb[k], 1), NT)
        return tuple(t_hi + t_lo)

    zero = jnp.zeros((1, DB), F32)
    terms = lax.fori_loop(0, 4, backward, (zero,) * 8)
    own_x = pltpu.make_async_copy(gseq.at[0], cols(out_x, rank), o_r.at[0])
    own_x.start()
    for j in range(2):
        for c in range(2):
            place = 2 * (side_hi + j - 2 * side_hi * j) + c
            sm_rep[rep, pl.ds(BLK + place, 1), :] = terms[2 * j + c]
            place = 2 * (side_lo + j - 2 * side_lo * j) + c
            sm_rep[rep, pl.ds(BLK + 4 + place, 1), :] = terms[4 + 2 * j + c]
    sm_rep[rep, BLK + 8 : BLK + 9, :] = gain_sum
    for step, other, to_dp, to_seq in replicas:
        sent.append(send(sm_rep.at[rep], sm_rep.at[rep], sr_s.at[step], sr_r.at[step], to_dp, to_seq))

    for step, other, to_dp, to_seq in replicas:
        source = (rep + reps - step) % reps
        arrived(gu_rep.at[source], gr_r.at[step])
        arrived(dn_rep.at[source], dr_r.at[step])
    gu_sum, dn_sum = gu_rep[0], dn_rep[0]
    for other in range(1, reps):
        gu_sum = gu_sum + gu_rep[other]
        dn_sum = dn_sum + dn_rep[other]
    gu_f32[...] = gu_sum * factor
    dn_f32[...] = dn_sum.T * factor
    for s in range(count):
        gu_out[s] = gu_f32[s * rows : (s + 1) * rows, :]
        dn_out[s] = dn_f32[s * drows : (s + 1) * drows, :]
    for k in ORDER:
        sent.append(send(gu_out.at[peer(k)], out_gu.at[rank], go_s.at[k], go_r.at[k], dp, peer(k)))
        sent.append(send(dn_out.at[peer(k)], out_dn.at[rank], do_s.at[k], do_r.at[k], dp, peer(k)))
    own = [
        own_x,
        pltpu.make_async_copy(gu_out.at[me], out_gu.at[rank], go_r.at[0]),
        pltpu.make_async_copy(dn_out.at[me], out_dn.at[rank], do_r.at[0]),
    ]
    own[1].start()
    own[2].start()

    for step, other, to_dp, to_seq in replicas:
        source = (rep + reps - step) % reps
        arrived(sm_rep.at[source], sr_r.at[step])
    sm_sum = sm_rep[0]
    for other in range(1, reps):
        sm_sum = sm_sum + sm_rep[other]
    sm_tot[...] = sm_sum * factor
    part = BLK // NB

    def part_of(rk):
        return sm_tot.at[pl.ds(pl.multiple_of(rk * part, part), part), :]

    for k in ORDER:
        sent.append(send(part_of(xor(rank, k, 4)), bm_in.at[k], bm_s.at[k], bm_r.at[k], dp, peer(k)))
    bm_sum = sm_tot[pl.ds(pl.multiple_of(rank * part, part), part), :]
    for k in range(1, NB):
        arrived(bm_in.at[k], bm_r.at[k])
        bm_sum = bm_sum + bm_in[k]
    pack[0:part, :] = bm_sum
    pack[part : part + SMALL, :] = sm_tot[BLK : BLK + SMALL, :]
    for k in ORDER:
        sent.append(send(pack, out_small.at[rank], pk_s.at[k], pk_r.at[k], dp, peer(k)))
    own.append(pltpu.make_async_copy(pack, out_small.at[rank], pk_r.at[0]))
    own[3].start()

    for copy in own:
        copy.wait()
    for k in range(1, NB):
        source = xor(rank, k, 4)
        arrived(out_gu.at[source], go_r.at[k])
        arrived(out_dn.at[source], do_r.at[k])
        arrived(cols(out_x, source), o_r.at[k])
        arrived(out_small.at[source], pk_r.at[k])
        arrived(gseq.at[k], o_s.at[k])
    for copy in sent:
        copy.wait_send()


def per_device(inputs, cotangent, block_mix, twist_hi, twist_lo, gain, gate_up, down):
    tokens, width = inputs.shape[1:]
    count = lax.axis_size("seq")
    dps = lax.axis_size("dp")
    groups = count // NB
    reps = dps * groups
    rows, drows = gate_up.shape[0], down.shape[0]
    factor = 1.0 / math.sqrt(dps * count * tokens)
    gu_rows = jnp.transpose(gate_up, (2, 0, 1, 3)).reshape(NB, rows, 2 * FB)
    dn_rows = jnp.transpose(down, (1, 0, 2))
    vmem = pl.BlockSpec(memory_space=pltpu.VMEM)
    hbm = pl.BlockSpec(memory_space=pl.ANY)
    dma = pltpu.SemaphoreType.DMA
    part = BLK // NB
    field = pltpu.VMEM((NB, tokens, DB), F32)
    many = max(count, reps)
    out_x, out_gu, out_dn, out_small = pl.pallas_call(
        functools.partial(kernel, dps, count, factor),
        out_shape=(
            jax.ShapeDtypeStruct((tokens, width), F32),
            jax.ShapeDtypeStruct((NB, rows, 2 * FB), F32),
            jax.ShapeDtypeStruct((NB, drows, DB), F32),
            jax.ShapeDtypeStruct((NB, part + SMALL, DB), F32),
        ),
        in_specs=[hbm, hbm, hbm, hbm, vmem, vmem, vmem, vmem],
        out_specs=(hbm, hbm, hbm, hbm),
        scratch_shapes=[field] * 8
        + [
            pltpu.VMEM((count, rows, 2 * FB), F32),
            pltpu.VMEM((count, drows, DB), F32),
            pltpu.VMEM((DB, 2 * FB), F32),
            pltpu.VMEM((FB, DB), F32),
            pltpu.VMEM((3 * DB, 2 * FB), BF16),
            pltpu.VMEM((DB, 6 * FB), BF16),
            pltpu.VMEM((FB, 3 * DB), BF16),
            pltpu.VMEM((reps, DB, 2 * FB), F32),
            pltpu.VMEM((reps, DB, FB), F32),
            pltpu.VMEM((count, rows, 2 * FB), F32),
            pltpu.VMEM((count, drows, DB), F32),
            pltpu.VMEM((reps, BLK + SMALL, DB), F32),
            pltpu.VMEM((BLK + SMALL, DB), F32),
            pltpu.VMEM((NB, part, DB), F32),
            pltpu.VMEM((part + SMALL, DB), F32),
            pltpu.VMEM((NB, NB, BLK), F32),
            pltpu.VMEM((NB, NB, BLK), F32),
            pltpu.VMEM((NB, BLK), F32),
        ]
        + [dma((many,))] * 28,
        compiler_params=pltpu.CompilerParams(
            collective_id=0, has_side_effects=True, vmem_limit_bytes=50 * 1024 * 1024
        ),
        name="butterfly_block",
    )(inputs[0], cotangent[0], gu_rows, dn_rows, block_mix, twist_hi, twist_lo, gain.reshape(1, width))
    grad_gu = jnp.transpose(out_gu.reshape(NB, rows, 2, FB), (1, 2, 0, 3))
    grad_dn = jnp.transpose(out_dn, (1, 0, 2))
    small = jnp.transpose(out_small[:, part:], (1, 0, 2)).reshape(SMALL, width)
    return (
        out_x[None],
        grad_gu,
        grad_dn,
        out_small[:, :part].reshape(BLK, BLK),
        small[0:4].reshape(2, 2, width),
        small[4:8].reshape(2, 2, width),
        small[8],
    )


def solution(mesh):
    return jax.shard_map(
        per_device,
        mesh=mesh,
        in_specs=(
            P("dp", "seq", None),
            P("dp", "seq", None),
            P(),
            P(),
            P(),
            P(),
            P("seq", None, None, None),
            P("seq", None, None),
        ),
        out_specs=(
            P("dp", "seq", None),
            P("seq", None, None, None),
            P("seq", None, None),
            P(),
            P(),
            P(),
            P(),
        ),
        check_vma=False,
    )
```

```python
import functools
import math

import jax
import jax.numpy as jnp
from jax import lax
from jax.experimental import pallas as pl
from jax.experimental.pallas import tpu as pltpu
from jax.sharding import PartitionSpec as P

NB = 16
BLK = 128
DB = 128
FB = 256
EPS = 1e-05
SMALL = 16
F32 = jnp.float32
BF16 = jnp.bfloat16
NN = (((1,), (0,)), ((), ()))
NT = (((1,), (1,)), ((), ()))
TN = (((0,), (0,)), ((), ()))
ORDER = (8, 1, 9, 2, 10, 3, 11, 4, 12, 5, 13, 6, 14, 7, 15)


def xor(a, b, bits):
    total = a + b
    for bit in range(bits):
        total = total - 2 * (1 << bit) * ((a // (1 << bit)) % 2) * ((b // (1 << bit)) % 2)
    return total


def split(value):
    high = value.astype(BF16)
    return high, (value - high.astype(F32)).astype(BF16)


def dot(a, b, dims):
    return lax.dot_general(a, b, dims, preferred_element_type=F32)


def left(value, axis):
    high, low = split(value)
    return jnp.concatenate([high, low, high], axis=axis)


def right(value, axis):
    high, low = split(value)
    return jnp.concatenate([high, high, low], axis=axis)


def row_sums(value):
    high, low = split(value)
    ones = jnp.ones((8, 2 * value.shape[1]), BF16)
    return dot(ones, jnp.concatenate([high, low], axis=1), NT)[0:1]


def as_columns(row):
    return jnp.broadcast_to(row, (DB, row.shape[1])).T


def arrived(ref, sem):
    pltpu.make_async_copy(ref, ref, sem).wait()


def kernel(
    dps, count, factor,
    x_hbm, g_hbm, gu_ref, dn_ref, bm_ref, th_ref, tl_ref, gain_ref,
    out_x, out_gu, out_dn, out_small,
    xb, gb, mixed, first, resid, scb, wsc, gseq,
    gu_blk, dn_blk, gu_in, dn_in, gu_f32, dn_f32, dn_t, gu_k, gu_n, dn_n,
    gu_part, dn_part, gu_rep, dn_rep, gu_out, dn_out, sm_rep, sm_tot, bm_in, pack,
    ss_buf, in_buf, rows_ref,
    x_s, x_r, g_s, g_r, gu_s, gu_r, dn_s, dn_r, ss_s, ss_r, in_s, in_r,
    o_s, o_r, gr_s, gr_r, dr_s, dr_r, go_s, go_r, do_s, do_r, sr_s, sr_r,
    bm_s, bm_r, pk_s, pk_r, wx_s, wx_r,
):
    groups = count // NB
    bits = count.bit_length() - 1
    reps = dps * groups
    rows, drows = DB // count, FB // count
    me = lax.axis_index("seq")
    dp = lax.axis_index("dp")
    rank = me % 2 + me // (2 * groups) * 2
    group = me // 2 % groups
    rep = dp * groups + group
    half = dp % 2
    pair = dp + 1 - 2 * half
    odd = (me + half) % 2

    def seq_of(rk, grp):
        return rk % 2 + grp * 2 + rk // 2 * 2 * groups

    def peer(k):
        return seq_of(xor(rank, k, 4), group)

    def send(src, dst, ssem, rsem, to_dp, to_seq):
        copy = pltpu.make_async_remote_copy(
            src_ref=src, dst_ref=dst, send_sem=ssem, recv_sem=rsem,
            device_id=(to_dp, to_seq), device_id_type=pl.DeviceIdType.MESH,
        )
        copy.start()
        return copy

    def cols(ref, rk):
        return ref.at[:, pl.ds(pl.multiple_of(rk * DB, DB), DB)]

    replicas = []
    for step in range(1, reps):
        other = (rep + step) % reps
        replicas.append((step, other, other // groups, seq_of(rank, other % groups)))

    barrier = pltpu.get_barrier_semaphore()
    met = 0
    for k in range(1, count):
        pl.semaphore_signal(
            barrier, inc=1, device_id=(dp, xor(me, k, bits)), device_id_type=pl.DeviceIdType.MESH
        )
        met += 1
    for step in range(1, dps):
        for grp in range(groups):
            pl.semaphore_signal(
                barrier, inc=1, device_id=((dp + step) % dps, seq_of(rank, grp)),
                device_id_type=pl.DeviceIdType.MESH,
            )
            met += 1
    pl.semaphore_wait(barrier, met)

    sent = []
    local = [
        pltpu.make_async_copy(cols(x_hbm, rank), xb.at[0], x_r.at[0]),
        pltpu.make_async_copy(cols(g_hbm, rank), gb.at[0], g_r.at[0]),
    ]
    for copy in local:
        copy.start()
    for k in ORDER:
        sent.append(send(cols(x_hbm, xor(rank, k, 4)), xb.at[k], x_s.at[k], x_r.at[k], dp, peer(k)))

    def weight_copies(k):
        to = xor(me, k, bits)
        block = to % 2 + to // (2 * groups) * 2
        slot = me // 2
        return [
            pltpu.make_async_remote_copy(
                src_ref=src.at[block], dst_ref=dst.at[half, slot], send_sem=ssem.at[k],
                recv_sem=rsem.at[k], device_id=(dp, to), device_id_type=pl.DeviceIdType.MESH,
            )
            for src, dst, ssem, rsem in ((gu_blk, gu_in, gu_s, gu_r), (dn_blk, dn_in, dn_s, dn_r))
        ]

    @pl.when(odd == 0)
    def _():
        for n in range(NB):
            for j in range(2):
                gu_blk[n, :, j * FB : (j + 1) * FB] = gu_ref[:, j, n, :]
            dn_blk[n] = dn_ref[:, n, :]
        pltpu.make_async_copy(gu_blk.at[rank], gu_in.at[half, me // 2], gu_r.at[0]).start()
        pltpu.make_async_copy(dn_blk.at[rank], dn_in.at[half, me // 2], dn_r.at[0]).start()
        for j in range(1, count):
            for copy in weight_copies(ORDER[j - 1] if count == NB else j):
                copy.start()

    mix_left = left(bm_ref[...], 1)
    back_left = left(bm_ref[...].T, 1)

    def mix(k, _):
        arrived(xb.at[k], x_r.at[k])
        mixed[k] = dot(mix_left, right(xb[k], 0), NN)
        return 0

    lax.fori_loop(0, NB // 2, mix, 0)
    for k in ORDER:
        sent.append(send(cols(g_hbm, xor(rank, k, 4)), gb.at[k], g_s.at[k], g_r.at[k], dp, peer(k)))
    lax.fori_loop(NB // 2, NB, mix, 0)

    lanes = pl.ds(pl.multiple_of(rank * DB, DB), DB)
    side_hi, side_lo = rank // 8, rank % 2

    def coefficients(ref, side):
        out = []
        for j in range(2):
            pair = ref[side + j - 2 * side * j, :, lanes]
            out.append((pair[0:1], pair[1:2]))
        return out

    hi = coefficients(th_ref, side_hi)
    lo = coefficients(tl_ref, side_lo)
    gain = gain_ref[:, lanes]

    def forward(i, _):
        ks = [2 * i, 2 * i + 1, 2 * i + 8, 2 * i + 9]
        mx = [mixed[k] for k in ks]
        fs = []
        for n in range(4):
            c = hi[n // 2]
            fs.append(c[0] * mx[n] + c[1] * mx[(n + 2) % 4])
            first[ks[n]] = fs[n]
        for n in range(4):
            c = lo[n % 2]
            r = xb[ks[n]] + (c[0] * fs[n] + c[1] * fs[n + 1 - 2 * (n % 2)])
            resid[ks[n]] = r
            ss_buf[0, pl.ds(xor(rank, ks[n], 4), 1), :] = row_sums(r * r)
        return 0

    lax.fori_loop(0, 4, forward, 0)
    for k in ORDER:
        sent.append(send(ss_buf.at[0], ss_buf.at[k], ss_s.at[k], ss_r.at[k], dp, peer(k)))

    for j in range(count // 2):
        k = 2 * j + odd
        owner = xor(me, k, bits)
        arrived(gu_in.at[half, owner // 2], gu_r.at[k])
        arrived(dn_in.at[half, owner // 2], dn_r.at[k])
    sent.append(send(gu_in.at[half], gu_in.at[half], wx_s.at[0], wx_r.at[0], pair, me))
    sent.append(send(dn_in.at[half], dn_in.at[half], wx_s.at[1], wx_r.at[1], pair, me))
    arrived(gu_in.at[1 - half], wx_r.at[0])
    arrived(dn_in.at[1 - half], wx_r.at[1])
    for s in range(count):
        gu_f32[s * rows : (s + 1) * rows, :] = gu_in[s % 2, s // 2]
        dn_f32[s * drows : (s + 1) * drows, :] = dn_in[s % 2, s // 2]
    gu_k[...] = right(gu_f32[...], 0)
    gu_n[...] = right(gu_f32[...], 1)
    dn_n[...] = right(dn_f32[...], 1)
    gu_f32[...] = jnp.zeros((DB, 2 * FB), F32)
    dn_t[...] = jnp.zeros((DB, FB), F32)

    for k in range(1, NB):
        arrived(ss_buf.at[k], ss_r.at[k])
    total = ss_buf[0]
    for k in range(1, NB):
        total = total + ss_buf[k]
    width = NB * DB
    rows_ref[...] = lax.rsqrt(total * (1.0 / width) + EPS)

    def mlp(i, gain_sum):
        scales, resids, cots = [], [], []
        for j in range(2):
            k = 2 * i + j
            arrived(gb.at[k], g_r.at[k])
            sc = as_columns(rows_ref[pl.ds(xor(rank, k, 4), 1), :])
            scb[k] = sc
            scales.append(sc)
            resids.append(resid[k])
            cots.append(gb[k])
        scale = jnp.concatenate(scales, axis=0)
        res = jnp.concatenate(resids, axis=0)
        cot = jnp.concatenate(cots, axis=0)
        unit = res * scale
        nh, nl = split(unit * gain)
        gh, gl = split(cot)
        gu = dot(jnp.concatenate([nh, nl, nh], axis=1), gu_k[...], NN)
        gate, up = gu[:, :FB], gu[:, FB:]
        sig = 1.0 / (1.0 + jnp.exp(-gate))
        act = gate * sig
        grad_hidden = dot(jnp.concatenate([gh, gl, gh], axis=1), dn_n[...], NT)
        hidden = right(act * up, 0)
        grad_gate = grad_hidden * up * sig * (1.0 + gate * (1.0 - sig))
        both_h, both_l = split(jnp.concatenate([grad_gate, grad_hidden * act], axis=1))
        grad_normed = dot(jnp.concatenate([both_h, both_l, both_h], axis=1), gu_n[...], NT)
        gu_f32[...] += dot(
            jnp.concatenate([nh, nl, nh], axis=0),
            jnp.concatenate([both_h, both_h, both_l], axis=0), TN,
        )
        dn_t[...] += dot(jnp.concatenate([gh, gl, gh], axis=0), hidden, TN)
        weighted = grad_normed * gain
        prod = weighted * res
        ws = weighted * scale
        for j in range(2):
            k = 2 * i + j
            wsc[k] = ws[j * BLK : (j + 1) * BLK]
            in_buf[0, pl.ds(xor(rank, k, 4), 1), :] = row_sums(prod[j * BLK : (j + 1) * BLK])
        return gain_sum + jnp.sum(grad_normed * unit, axis=0, keepdims=True)

    gain_sum = lax.fori_loop(0, NB // 2, mlp, jnp.zeros((1, DB), F32))

    for k in ORDER:
        sent.append(send(in_buf.at[0], in_buf.at[k], in_s.at[k], in_r.at[k], dp, peer(k)))
    dn_f32[...] = dn_t[...].T
    for s in range(count):
        gu_part[s % 2, s // 2] = gu_f32[s * rows : (s + 1) * rows, :]
        dn_part[s % 2, s // 2] = dn_f32[s * drows : (s + 1) * drows, :]
    for step, other, to_dp, to_seq in replicas:
        theirs = to_dp % 2
        sent.append(send(gu_part.at[theirs], gu_rep.at[rep], gr_s.at[step], gr_r.at[step], to_dp, to_seq))
        sent.append(send(dn_part.at[theirs], dn_rep.at[rep], dr_s.at[step], dr_r.at[step], to_dp, to_seq))
    gu_rep[rep] = gu_part[half]
    dn_rep[rep] = dn_part[half]

    for k in range(1, NB):
        arrived(in_buf.at[k], in_r.at[k])
    total = in_buf[0]
    for k in range(1, NB):
        total = total + in_buf[k]
    rows_ref[...] = total * (1.0 / width)

    for step, other, to_dp, to_seq in replicas:
        source = (rep + reps - step) % reps
        arrived(gu_rep.at[source], gr_r.at[step])
        arrived(dn_rep.at[source], dr_r.at[step])
    gu_sum, dn_sum = gu_rep[0], dn_rep[0]
    for other in range(1, reps):
        gu_sum = gu_sum + gu_rep[other]
        dn_sum = dn_sum + dn_rep[other]
    gu_out[...] = gu_sum * factor
    dn_out[...] = dn_sum * factor

    def grad_copies(k):
        to = peer(k)
        return [
            pltpu.make_async_remote_copy(
                src_ref=src.at[to // 2], dst_ref=dst.at[rank], send_sem=ssem.at[k],
                recv_sem=rsem.at[k], device_id=(dp, to), device_id_type=pl.DeviceIdType.MESH,
            )
            for src, dst, ssem, rsem in ((gu_out, out_gu, go_s, go_r), (dn_out, out_dn, do_s, do_r))
        ]

    swap = [
        pltpu.make_async_remote_copy(
            src_ref=ref, dst_ref=ref, send_sem=wx_s.at[n], recv_sem=wx_r.at[n],
            device_id=(pair, me), device_id_type=pl.DeviceIdType.MESH,
        )
        for n, ref in ((2, out_gu), (3, out_dn))
    ]

    @pl.when(odd == 0)
    def _():
        pltpu.make_async_copy(gu_out.at[me // 2], out_gu.at[rank], go_r.at[0]).start()
        pltpu.make_async_copy(dn_out.at[me // 2], out_dn.at[rank], do_r.at[0]).start()

    for j in reversed(range(NB // 2)):
        k = 2 * j + odd

        @pl.when(k != 0)
        def _():
            for copy in grad_copies(k):
                copy.start()

    sm_rep[rep] = jnp.zeros((BLK + SMALL, DB), F32)

    def backward(i, carry):
        q = 3 - i
        ks = [2 * q, 2 * q + 1, 2 * q + 8, 2 * q + 9]
        t_hi, t_lo = list(carry[:4]), list(carry[4:])
        gr = []
        for k in ks:
            inner = as_columns(rows_ref[pl.ds(xor(rank, k, 4), 1), :])
            sc = scb[k]
            gr.append(gb[k] + wsc[k] - resid[k] * sc * sc * sc * inner)
        fs = [first[k] for k in ks]
        mx = [mixed[k] for k in ks]
        gf = []
        for n in range(4):
            j, m = n % 2, n + 1 - 2 * (n % 2)
            gf.append(lo[j][0] * gr[n] + lo[1 - j][1] * gr[m])
            t_lo[2 * j] += jnp.sum(gr[n] * fs[n], axis=0, keepdims=True)
            t_lo[2 * j + 1] += jnp.sum(gr[n] * fs[m], axis=0, keepdims=True)
        for n in range(4):
            j, m = n // 2, (n + 2) % 4
            gm = hi[j][0] * gf[n] + hi[1 - j][1] * gf[m]
            t_hi[2 * j] += jnp.sum(gf[n] * mx[n], axis=0, keepdims=True)
            t_hi[2 * j + 1] += jnp.sum(gf[n] * mx[m], axis=0, keepdims=True)
            mh, ml = split(gm)
            gseq[ks[n]] = dot(back_left, jnp.concatenate([mh, mh, ml], axis=0), NN) + gr[n]
            k = ks[n]

            @pl.when(k != 0)
            def _():
                send(gseq.at[k], cols(out_x, rank), o_s.at[k], o_r.at[k], dp, peer(k))

            sm_rep[rep, :BLK, :] += dot(jnp.concatenate([mh, ml, mh], axis=1), right(xb[k], 1), NT)
        return tuple(t_hi + t_lo)

    zero = jnp.zeros((1, DB), F32)
    terms = lax.fori_loop(0, 4, backward, (zero,) * 8)
    own_x = pltpu.make_async_copy(gseq.at[0], cols(out_x, rank), o_r.at[0])
    own_x.start()
    for j in range(2):
        for c in range(2):
            place = 2 * (side_hi + j - 2 * side_hi * j) + c
            sm_rep[rep, pl.ds(BLK + place, 1), :] = terms[2 * j + c]
            place = 2 * (side_lo + j - 2 * side_lo * j) + c
            sm_rep[rep, pl.ds(BLK + 4 + place, 1), :] = terms[4 + 2 * j + c]
    sm_rep[rep, BLK + 8 : BLK + 9, :] = gain_sum
    for step, other, to_dp, to_seq in replicas:
        sent.append(send(sm_rep.at[rep], sm_rep.at[rep], sr_s.at[step], sr_r.at[step], to_dp, to_seq))

    @pl.when(odd == 0)
    def _():
        for k in range(NB):
            source = xor(rank, k, 4)
            arrived(out_gu.at[source], go_r.at[k])
            arrived(out_dn.at[source], do_r.at[k])
        for copy in swap:
            copy.start()

    for step, other, to_dp, to_seq in replicas:
        source = (rep + reps - step) % reps
        arrived(sm_rep.at[source], sr_r.at[step])
    sm_sum = sm_rep[0]
    for other in range(1, reps):
        sm_sum = sm_sum + sm_rep[other]
    sm_tot[...] = sm_sum * factor
    part = BLK // NB

    def part_of(rk):
        return sm_tot.at[pl.ds(pl.multiple_of(rk * part, part), part), :]

    for k in ORDER:
        sent.append(send(part_of(xor(rank, k, 4)), bm_in.at[k], bm_s.at[k], bm_r.at[k], dp, peer(k)))
    bm_sum = sm_tot[pl.ds(pl.multiple_of(rank * part, part), part), :]
    for k in range(1, NB):
        arrived(bm_in.at[k], bm_r.at[k])
        bm_sum = bm_sum + bm_in[k]
    pack[0:part, :] = bm_sum
    pack[part : part + SMALL, :] = sm_tot[BLK : BLK + SMALL, :]
    for k in ORDER:
        sent.append(send(pack, out_small.at[rank], pk_s.at[k], pk_r.at[k], dp, peer(k)))
    own = [own_x, pltpu.make_async_copy(pack, out_small.at[rank], pk_r.at[0])]
    own[1].start()

    for copy in own:
        copy.wait()
    for k in range(1, NB):
        source = xor(rank, k, 4)
        arrived(cols(out_x, source), o_r.at[k])
        arrived(out_small.at[source], pk_r.at[k])
        arrived(gseq.at[k], o_s.at[k])
    for copy in sent:
        copy.wait_send()

    @pl.when(odd == 0)
    def _():
        for copy in swap:
            copy.wait_send()
        for k in range(1, count):
            for copy in weight_copies(k):
                copy.wait_send()

    @pl.when(odd == 1)
    def _():
        for copy in swap:
            copy.wait_recv()

    for j in range(NB // 2):
        k = 2 * j + odd

        @pl.when(k != 0)
        def _():
            for copy in grad_copies(k):
                copy.wait_send()


def per_device(inputs, cotangent, block_mix, twist_hi, twist_lo, gain, gate_up, down):
    tokens, width = inputs.shape[1:]
    count = lax.axis_size("seq")
    dps = lax.axis_size("dp")
    groups = count // NB
    reps = dps * groups
    rows, drows = gate_up.shape[0], down.shape[0]
    factor = 1.0 / math.sqrt(dps * count * tokens)
    vmem = pl.BlockSpec(memory_space=pltpu.VMEM)
    hbm = pl.BlockSpec(memory_space=pl.ANY)
    dma = pltpu.SemaphoreType.DMA
    part = BLK // NB
    field = pltpu.VMEM((NB, tokens, DB), F32)
    many = max(count, reps)
    out_x, out_gu, out_dn, out_small = pl.pallas_call(
        functools.partial(kernel, dps, count, factor),
        out_shape=(
            jax.ShapeDtypeStruct((tokens, width), F32),
            jax.ShapeDtypeStruct((NB, rows, 2 * FB), F32),
            jax.ShapeDtypeStruct((NB, drows, DB), F32),
            jax.ShapeDtypeStruct((NB, part + SMALL, DB), F32),
        ),
        in_specs=[hbm, hbm] + [vmem] * 6,
        out_specs=(hbm, hbm, hbm, hbm),
        scratch_shapes=[field] * 8
        + [
            pltpu.VMEM((NB, rows, 2 * FB), F32),
            pltpu.VMEM((NB, drows, DB), F32),
            pltpu.VMEM((2, count // 2, rows, 2 * FB), F32),
            pltpu.VMEM((2, count // 2, drows, DB), F32),
            pltpu.VMEM((DB, 2 * FB), F32),
            pltpu.VMEM((FB, DB), F32),
            pltpu.VMEM((DB, FB), F32),
            pltpu.VMEM((3 * DB, 2 * FB), BF16),
            pltpu.VMEM((DB, 6 * FB), BF16),
            pltpu.VMEM((FB, 3 * DB), BF16),
            pltpu.VMEM((2, count // 2, rows, 2 * FB), F32),
            pltpu.VMEM((2, count // 2, drows, DB), F32),
            pltpu.VMEM((reps, count // 2, rows, 2 * FB), F32),
            pltpu.VMEM((reps, count // 2, drows, DB), F32),
            pltpu.VMEM((count // 2, rows, 2 * FB), F32),
            pltpu.VMEM((count // 2, drows, DB), F32),
            pltpu.VMEM((reps, BLK + SMALL, DB), F32),
            pltpu.VMEM((BLK + SMALL, DB), F32),
            pltpu.VMEM((NB, part, DB), F32),
            pltpu.VMEM((part + SMALL, DB), F32),
            pltpu.VMEM((NB, NB, BLK), F32),
            pltpu.VMEM((NB, NB, BLK), F32),
            pltpu.VMEM((NB, BLK), F32),
        ]
        + [dma((many,))] * 30,
        compiler_params=pltpu.CompilerParams(
            collective_id=0, has_side_effects=True, vmem_limit_bytes=50 * 1024 * 1024
        ),
        name="butterfly_block",
    )(inputs[0], cotangent[0], gate_up, down, block_mix, twist_hi, twist_lo, gain.reshape(1, width))
    grad_gu = jnp.transpose(out_gu.reshape(NB, rows, 2, FB), (1, 2, 0, 3))
    grad_dn = jnp.transpose(out_dn, (1, 0, 2))
    small = jnp.transpose(out_small[:, part:], (1, 0, 2)).reshape(SMALL, width)
    return (
        out_x[None],
        grad_gu,
        grad_dn,
        out_small[:, :part].reshape(BLK, BLK),
        small[0:4].reshape(2, 2, width),
        small[4:8].reshape(2, 2, width),
        small[8],
    )


def solution(mesh):
    return jax.shard_map(
        per_device,
        mesh=mesh,
        in_specs=(
            P("dp", "seq", None),
            P("dp", "seq", None),
            P(),
            P(),
            P(),
            P(),
            P("seq", None, None, None),
            P("seq", None, None),
        ),
        out_specs=(
            P("dp", "seq", None),
            P("seq", None, None, None),
            P("seq", None, None),
            P(),
            P(),
            P(),
            P(),
        ),
        check_vma=False,
    )
```

```python
import functools
import math

import jax
import jax.numpy as jnp
from jax import lax
from jax.experimental import pallas as pl
from jax.experimental.pallas import tpu as pltpu
from jax.sharding import PartitionSpec as P

NB = 16
BLK = 128
DB = 128
FB = 256
EPS = 1e-05
SMALL = 16
PIECES = 4
VMEM_LIMIT = 60 * 1024 * 1024
F32 = jnp.float32
BF16 = jnp.bfloat16
NN = (((1,), (0,)), ((), ()))
NT = (((1,), (1,)), ((), ()))
TN = (((0,), (0,)), ((), ()))
ORDER = (8, 1, 9, 2, 10, 3, 11, 4, 12, 5, 13, 6, 14, 7, 15)


def xor(a, b, bits):
    total = a + b
    for bit in range(bits):
        total = total - 2 * (1 << bit) * ((a // (1 << bit)) % 2) * ((b // (1 << bit)) % 2)
    return total


def split(value):
    high = value.astype(BF16)
    return high, (value - high.astype(F32)).astype(BF16)


def dot(a, b, dims):
    return lax.dot_general(a, b, dims, preferred_element_type=F32)


def left(value, axis):
    high, low = split(value)
    return jnp.concatenate([high, low, high], axis=axis)


def right(value, axis):
    high, low = split(value)
    return jnp.concatenate([high, high, low], axis=axis)


def row_sums(value):
    high, low = split(value)
    ones = jnp.ones((8, 2 * value.shape[1]), BF16)
    return dot(ones, jnp.concatenate([high, low], axis=1), NT)[0:1]


def as_columns(row):
    return jnp.broadcast_to(row, (DB, row.shape[1])).T


def arrived(ref, sem):
    pltpu.make_async_copy(ref, ref, sem).wait()


def kernel(
    dps, count, factor,
    x_hbm, g_hbm, gu_hbm, dn_hbm, bm_hbm, th_hbm, tl_hbm, gain_hbm,
    out_x, out_gu, out_dn, out_small,
    xb, gb, mixed, first, resid, scb, wsc, gseq,
    gu_ref, dn_ref, bm_ref, th_ref, tl_ref, gain_ref,
    gu_blk, dn_blk, gu_in, dn_in, gu_f32, dn_f32, dn_t, gu_k, gu_n, dn_n,
    gu_part, dn_part, gu_rep, dn_rep, gu_out, dn_out, sm_rep, sm_tot, bm_in, pack,
    ss_buf, in_buf, rows_ref,
    x_s, x_r, g_s, g_r, gu_s, gu_r, dn_s, dn_r, ss_s, ss_r, in_s, in_r,
    o_s, o_r, gr_s, gr_r, dr_s, dr_r, go_s, go_r, do_s, do_r, sr_s, sr_r,
    bm_s, bm_r, pk_s, pk_r, wx_s, wx_r, p_r,
):
    groups = count // NB
    bits = count.bit_length() - 1
    reps = dps * groups
    rows, drows = DB // count, FB // count
    me = lax.axis_index("seq")
    dp = lax.axis_index("dp")
    rank = me % 2 + me // (2 * groups) * 2
    group = me // 2 % groups
    rep = dp * groups + group
    half = dp % 2
    pair = dp + 1 - 2 * half
    odd = (me + half) % 2

    def seq_of(rk, grp):
        return rk % 2 + grp * 2 + rk // 2 * 2 * groups

    def peer(k):
        return seq_of(xor(rank, k, 4), group)

    def send(src, dst, ssem, rsem, to_dp, to_seq):
        copy = pltpu.make_async_remote_copy(
            src_ref=src, dst_ref=dst, send_sem=ssem, recv_sem=rsem,
            device_id=(to_dp, to_seq), device_id_type=pl.DeviceIdType.MESH,
        )
        copy.start()
        return copy

    def cols(ref, rk):
        return ref.at[:, pl.ds(pl.multiple_of(rk * DB, DB), DB)]

    replicas = []
    for step in range(1, reps):
        other = (rep + step) % reps
        replicas.append((step, other, other // groups, seq_of(rank, other % groups)))

    params = [
        pltpu.make_async_copy(src, dst, p_r.at[n])
        for n, (src, dst) in enumerate((
            (bm_hbm, bm_ref), (gu_hbm, gu_ref), (dn_hbm, dn_ref),
            (th_hbm, th_ref), (tl_hbm, tl_ref), (gain_hbm, gain_ref),
        ))
    ]
    local = [
        pltpu.make_async_copy(cols(x_hbm, rank), xb.at[0], x_r.at[0]),
        pltpu.make_async_copy(cols(g_hbm, rank), gb.at[0], g_r.at[0]),
    ]
    for copy in params + local:
        copy.start()

    barrier = pltpu.get_barrier_semaphore()
    met = 0
    for k in range(1, count):
        pl.semaphore_signal(
            barrier, inc=1, device_id=(dp, xor(me, k, bits)), device_id_type=pl.DeviceIdType.MESH
        )
        met += 1
    for step in range(1, dps):
        for grp in range(groups):
            pl.semaphore_signal(
                barrier, inc=1, device_id=((dp + step) % dps, seq_of(rank, grp)),
                device_id_type=pl.DeviceIdType.MESH,
            )
            met += 1
    pl.semaphore_wait(barrier, met)

    sent = []
    for k in ORDER:
        sent.append(send(cols(x_hbm, xor(rank, k, 4)), xb.at[k], x_s.at[k], x_r.at[k], dp, peer(k)))

    for copy in params:
        copy.wait()

    def weight_copies(k):
        to = xor(me, k, bits)
        block = to % 2 + to // (2 * groups) * 2
        slot = me // 2
        return [
            pltpu.make_async_remote_copy(
                src_ref=src.at[block], dst_ref=dst.at[half, slot], send_sem=ssem.at[k],
                recv_sem=rsem.at[k], device_id=(dp, to), device_id_type=pl.DeviceIdType.MESH,
            )
            for src, dst, ssem, rsem in ((gu_blk, gu_in, gu_s, gu_r), (dn_blk, dn_in, dn_s, dn_r))
        ]

    @pl.when(odd == 0)
    def _():
        for n in range(NB):
            for j in range(2):
                gu_blk[n, :, j * FB : (j + 1) * FB] = gu_ref[:, j, n, :]
            dn_blk[n] = dn_ref[:, n, :]
        pltpu.make_async_copy(gu_blk.at[rank], gu_in.at[half, me // 2], gu_r.at[0]).start()
        pltpu.make_async_copy(dn_blk.at[rank], dn_in.at[half, me // 2], dn_r.at[0]).start()
        for j in range(1, count):
            for copy in weight_copies(ORDER[j - 1] if count == NB else j):
                copy.start()

    mix_left = left(bm_ref[...], 1)
    back_left = left(bm_ref[...].T, 1)

    def mix(k, _):
        arrived(xb.at[k], x_r.at[k])
        mixed[k] = dot(mix_left, right(xb[k], 0), NN)
        return 0

    lax.fori_loop(0, NB // 2, mix, 0)
    for k in ORDER:
        sent.append(send(cols(g_hbm, xor(rank, k, 4)), gb.at[k], g_s.at[k], g_r.at[k], dp, peer(k)))
    lax.fori_loop(NB // 2, NB, mix, 0)

    lanes = pl.ds(pl.multiple_of(rank * DB, DB), DB)
    side_hi, side_lo = rank // 8, rank % 2

    def coefficients(ref, side):
        out = []
        for j in range(2):
            pair = ref[side + j - 2 * side * j, :, lanes]
            out.append((pair[0:1], pair[1:2]))
        return out

    hi = coefficients(th_ref, side_hi)
    lo = coefficients(tl_ref, side_lo)
    gain = gain_ref[:, lanes]

    def forward(i, _):
        ks = [2 * i, 2 * i + 1, 2 * i + 8, 2 * i + 9]
        mx = [mixed[k] for k in ks]
        fs = []
        for n in range(4):
            c = hi[n // 2]
            fs.append(c[0] * mx[n] + c[1] * mx[(n + 2) % 4])
            first[ks[n]] = fs[n]
        for n in range(4):
            c = lo[n % 2]
            r = xb[ks[n]] + (c[0] * fs[n] + c[1] * fs[n + 1 - 2 * (n % 2)])
            resid[ks[n]] = r
            ss_buf[0, pl.ds(xor(rank, ks[n], 4), 1), :] = row_sums(r * r)
        return 0

    lax.fori_loop(0, 4, forward, 0)
    for k in ORDER:
        sent.append(send(ss_buf.at[0], ss_buf.at[k], ss_s.at[k], ss_r.at[k], dp, peer(k)))

    for j in range(count // 2):
        k = 2 * j + odd
        owner = xor(me, k, bits)
        arrived(gu_in.at[half, owner // 2], gu_r.at[k])
        arrived(dn_in.at[half, owner // 2], dn_r.at[k])
    sent.append(send(gu_in.at[half], gu_in.at[half], wx_s.at[0], wx_r.at[0], pair, me))
    sent.append(send(dn_in.at[half], dn_in.at[half], wx_s.at[1], wx_r.at[1], pair, me))
    arrived(gu_in.at[1 - half], wx_r.at[0])
    arrived(dn_in.at[1 - half], wx_r.at[1])
    for s in range(count):
        gu_f32[s * rows : (s + 1) * rows, :] = gu_in[s % 2, s // 2]
        dn_f32[s * drows : (s + 1) * drows, :] = dn_in[s % 2, s // 2]
    gu_k[...] = right(gu_f32[...], 0)
    gu_n[...] = right(gu_f32[...], 1)
    dn_n[...] = right(dn_f32[...], 1)
    gu_f32[...] = jnp.zeros((DB, 2 * FB), F32)
    dn_t[...] = jnp.zeros((DB, FB), F32)

    for k in range(1, NB):
        arrived(ss_buf.at[k], ss_r.at[k])
    total = ss_buf[0]
    for k in range(1, NB):
        total = total + ss_buf[k]
    width = NB * DB
    rows_ref[...] = lax.rsqrt(total * (1.0 / width) + EPS)

    def mlp(i, gain_sum):
        scales, resids, cots = [], [], []
        for j in range(2):
            k = 2 * i + j
            arrived(gb.at[k], g_r.at[k])
            sc = as_columns(rows_ref[pl.ds(xor(rank, k, 4), 1), :])
            scb[k] = sc
            scales.append(sc)
            resids.append(resid[k])
            cots.append(gb[k])
        scale = jnp.concatenate(scales, axis=0)
        res = jnp.concatenate(resids, axis=0)
        cot = jnp.concatenate(cots, axis=0)
        unit = res * scale
        nh, nl = split(unit * gain)
        gh, gl = split(cot)
        gu = dot(jnp.concatenate([nh, nl, nh], axis=1), gu_k[...], NN)
        gate, up = gu[:, :FB], gu[:, FB:]
        sig = 1.0 / (1.0 + jnp.exp(-gate))
        act = gate * sig
        grad_hidden = dot(jnp.concatenate([gh, gl, gh], axis=1), dn_n[...], NT)
        hidden = right(act * up, 0)
        grad_gate = grad_hidden * up * sig * (1.0 + gate * (1.0 - sig))
        both_h, both_l = split(jnp.concatenate([grad_gate, grad_hidden * act], axis=1))
        grad_normed = dot(jnp.concatenate([both_h, both_l, both_h], axis=1), gu_n[...], NT)
        gu_f32[...] += dot(
            jnp.concatenate([nh, nl, nh], axis=0),
            jnp.concatenate([both_h, both_h, both_l], axis=0), TN,
        )
        dn_t[...] += dot(jnp.concatenate([gh, gl, gh], axis=0), hidden, TN)
        weighted = grad_normed * gain
        prod = weighted * res
        ws = weighted * scale
        for j in range(2):
            k = 2 * i + j
            wsc[k] = ws[j * BLK : (j + 1) * BLK]
            in_buf[0, pl.ds(xor(rank, k, 4), 1), :] = row_sums(prod[j * BLK : (j + 1) * BLK])
        return gain_sum + jnp.sum(grad_normed * unit, axis=0, keepdims=True)

    gain_sum = lax.fori_loop(0, NB // 2, mlp, jnp.zeros((1, DB), F32))

    for k in ORDER:
        sent.append(send(in_buf.at[0], in_buf.at[k], in_s.at[k], in_r.at[k], dp, peer(k)))
    dn_f32[...] = dn_t[...].T
    for s in range(count):
        gu_part[s % 2, s // 2] = gu_f32[s * rows : (s + 1) * rows, :]
        dn_part[s % 2, s // 2] = dn_f32[s * drows : (s + 1) * drows, :]
    for step, other, to_dp, to_seq in replicas:
        theirs = to_dp % 2
        sent.append(send(gu_part.at[theirs], gu_rep.at[rep], gr_s.at[step], gr_r.at[step], to_dp, to_seq))
        sent.append(send(dn_part.at[theirs], dn_rep.at[rep], dr_s.at[step], dr_r.at[step], to_dp, to_seq))
    gu_rep[rep] = gu_part[half]
    dn_rep[rep] = dn_part[half]

    for k in range(1, NB):
        arrived(in_buf.at[k], in_r.at[k])
    total = in_buf[0]
    for k in range(1, NB):
        total = total + in_buf[k]
    rows_ref[...] = total * (1.0 / width)

    sm_rep[rep] = jnp.zeros((BLK + SMALL, DB), F32)

    def backward(i, carry):
        q = 3 - i
        ks = [2 * q, 2 * q + 1, 2 * q + 8, 2 * q + 9]
        t_hi, t_lo = list(carry[:4]), list(carry[4:])
        gr = []
        for k in ks:
            inner = as_columns(rows_ref[pl.ds(xor(rank, k, 4), 1), :])
            sc = scb[k]
            gr.append(gb[k] + wsc[k] - resid[k] * sc * sc * sc * inner)
        fs = [first[k] for k in ks]
        mx = [mixed[k] for k in ks]
        gf = []
        for n in range(4):
            j, m = n % 2, n + 1 - 2 * (n % 2)
            gf.append(lo[j][0] * gr[n] + lo[1 - j][1] * gr[m])
            t_lo[2 * j] += jnp.sum(gr[n] * fs[n], axis=0, keepdims=True)
            t_lo[2 * j + 1] += jnp.sum(gr[n] * fs[m], axis=0, keepdims=True)
        for n in range(4):
            j, m = n // 2, (n + 2) % 4
            gm = hi[j][0] * gf[n] + hi[1 - j][1] * gf[m]
            t_hi[2 * j] += jnp.sum(gf[n] * mx[n], axis=0, keepdims=True)
            t_hi[2 * j + 1] += jnp.sum(gf[n] * mx[m], axis=0, keepdims=True)
            mh, ml = split(gm)
            gseq[ks[n]] = dot(back_left, jnp.concatenate([mh, mh, ml], axis=0), NN) + gr[n]
            k = ks[n]

            @pl.when(k != 0)
            def _():
                send(gseq.at[k], cols(out_x, rank), o_s.at[k], o_r.at[k], dp, peer(k))

            sm_rep[rep, :BLK, :] += dot(jnp.concatenate([mh, ml, mh], axis=1), right(xb[k], 1), NT)
        return tuple(t_hi + t_lo)

    zero = jnp.zeros((1, DB), F32)
    terms = lax.fori_loop(0, 2, backward, (zero,) * 8)

    for step, other, to_dp, to_seq in replicas:
        source = (rep + reps - step) % reps
        arrived(gu_rep.at[source], gr_r.at[step])
        arrived(dn_rep.at[source], dr_r.at[step])
    gu_sum, dn_sum = gu_rep[0], dn_rep[0]
    for other in range(1, reps):
        gu_sum = gu_sum + gu_rep[other]
        dn_sum = dn_sum + dn_rep[other]
    gu_out[...] = gu_sum * factor
    dn_out[...] = dn_sum * factor

    def grad_copies(k):
        to = peer(k)
        return [
            pltpu.make_async_remote_copy(
                src_ref=src.at[to // 2], dst_ref=dst.at[rank], send_sem=ssem.at[k],
                recv_sem=rsem.at[k], device_id=(dp, to), device_id_type=pl.DeviceIdType.MESH,
            )
            for src, dst, ssem, rsem in ((gu_out, out_gu, go_s, go_r), (dn_out, out_dn, do_s, do_r))
        ]

    swap = [
        pltpu.make_async_remote_copy(
            src_ref=ref, dst_ref=ref, send_sem=wx_s.at[n], recv_sem=wx_r.at[n],
            device_id=(pair, me), device_id_type=pl.DeviceIdType.MESH,
        )
        for n, ref in ((2, out_gu), (3, out_dn))
    ]

    @pl.when(odd == 0)
    def _():
        pltpu.make_async_copy(gu_out.at[me // 2], out_gu.at[rank], go_r.at[0]).start()
        pltpu.make_async_copy(dn_out.at[me // 2], out_dn.at[rank], do_r.at[0]).start()

    for j in reversed(range(NB // 2)):
        k = 2 * j + odd

        @pl.when(k != 0)
        def _():
            for copy in grad_copies(k):
                copy.start()

    terms = lax.fori_loop(2, 4, backward, terms)
    own_x = pltpu.make_async_copy(gseq.at[0], cols(out_x, rank), o_r.at[0])
    own_x.start()
    for j in range(2):
        for c in range(2):
            place = 2 * (side_hi + j - 2 * side_hi * j) + c
            sm_rep[rep, pl.ds(BLK + place, 1), :] = terms[2 * j + c]
            place = 2 * (side_lo + j - 2 * side_lo * j) + c
            sm_rep[rep, pl.ds(BLK + 4 + place, 1), :] = terms[4 + 2 * j + c]
    sm_rep[rep, BLK + 8 : BLK + 9, :] = gain_sum
    for step, other, to_dp, to_seq in replicas:
        sent.append(send(sm_rep.at[rep], sm_rep.at[rep], sr_s.at[step], sr_r.at[step], to_dp, to_seq))

    @pl.when(odd == 0)
    def _():
        for k in range(NB):
            source = xor(rank, k, 4)
            arrived(out_gu.at[source], go_r.at[k])
            arrived(out_dn.at[source], do_r.at[k])
        for copy in swap:
            copy.start()

    for step, other, to_dp, to_seq in replicas:
        source = (rep + reps - step) % reps
        arrived(sm_rep.at[source], sr_r.at[step])
    sm_sum = sm_rep[0]
    for other in range(1, reps):
        sm_sum = sm_sum + sm_rep[other]
    sm_tot[...] = sm_sum * factor
    part = BLK // NB

    def part_of(rk):
        return sm_tot.at[pl.ds(pl.multiple_of(rk * part, part), part), :]

    for k in ORDER:
        sent.append(send(part_of(xor(rank, k, 4)), bm_in.at[k], bm_s.at[k], bm_r.at[k], dp, peer(k)))
    bm_sum = sm_tot[pl.ds(pl.multiple_of(rank * part, part), part), :]
    for k in range(1, NB):
        arrived(bm_in.at[k], bm_r.at[k])
        bm_sum = bm_sum + bm_in[k]
    pack[0:part, :] = bm_sum
    pack[part : part + SMALL, :] = sm_tot[BLK : BLK + SMALL, :]
    for k in ORDER:
        sent.append(send(pack, out_small.at[rank], pk_s.at[k], pk_r.at[k], dp, peer(k)))
    own = [own_x, pltpu.make_async_copy(pack, out_small.at[rank], pk_r.at[0])]
    own[1].start()

    for copy in own:
        copy.wait()
    for k in range(1, NB):
        source = xor(rank, k, 4)
        arrived(cols(out_x, source), o_r.at[k])
        arrived(out_small.at[source], pk_r.at[k])
        arrived(gseq.at[k], o_s.at[k])
    for copy in sent:
        copy.wait_send()

    @pl.when(odd == 0)
    def _():
        for copy in swap:
            copy.wait_send()
        for k in range(1, count):
            for copy in weight_copies(k):
                copy.wait_send()

    @pl.when(odd == 1)
    def _():
        for copy in swap:
            copy.wait_recv()

    for j in range(NB // 2):
        k = 2 * j + odd

        @pl.when(k != 0)
        def _():
            for copy in grad_copies(k):
                copy.wait_send()


def lay_out(x_in, gu_in, dn_in, small, x_out, gu_out, dn_out, bm_out, th_out, tl_out, gain_out, sem):
    rows = x_in.shape[0] // PIECES
    copies = [
        pltpu.make_async_copy(
            x_in.at[n * rows : (n + 1) * rows], x_out.at[n * rows : (n + 1) * rows], sem.at[n]
        )
        for n in range(PIECES)
    ]
    for copy in copies:
        copy.start()
    part = BLK // NB
    for n in range(NB):
        lanes = slice(n * DB, (n + 1) * DB)
        for j in range(2):
            gu_out[:, j, n, :] = gu_in[n, :, j * FB : (j + 1) * FB]
            th_out[j, :, lanes] = small[n, part + 2 * j : part + 2 * j + 2, :]
            tl_out[j, :, lanes] = small[n, part + 4 + 2 * j : part + 6 + 2 * j, :]
        dn_out[:, n, :] = dn_in[n]
        bm_out[n * part : (n + 1) * part, :] = small[n, 0:part, :]
        gain_out[:, lanes] = small[n, part + 8 : part + 9, :]
    for copy in copies:
        copy.wait()


def per_device(inputs, cotangent, block_mix, twist_hi, twist_lo, gain, gate_up, down):
    tokens, width = inputs.shape[1:]
    count = lax.axis_size("seq")
    dps = lax.axis_size("dp")
    groups = count // NB
    reps = dps * groups
    rows, drows = gate_up.shape[0], down.shape[0]
    factor = 1.0 / math.sqrt(dps * count * tokens)
    vmem = pl.BlockSpec(memory_space=pltpu.VMEM)
    hbm = pl.BlockSpec(memory_space=pl.ANY)
    dma = pltpu.SemaphoreType.DMA
    part = BLK // NB
    field = pltpu.VMEM((NB, tokens, DB), F32)
    many = max(count, reps)
    out_x, out_gu, out_dn, out_small = pl.pallas_call(
        functools.partial(kernel, dps, count, factor),
        out_shape=(
            jax.ShapeDtypeStruct((tokens, width), F32),
            jax.ShapeDtypeStruct((NB, rows, 2 * FB), F32),
            jax.ShapeDtypeStruct((NB, drows, DB), F32),
            jax.ShapeDtypeStruct((NB, part + SMALL, DB), F32),
        ),
        in_specs=[pl.BlockSpec(memory_space=pltpu.HBM)] * 8,
        out_specs=(hbm, hbm, hbm, hbm),
        scratch_shapes=[field] * 8
        + [
            pltpu.VMEM(gate_up.shape, F32),
            pltpu.VMEM(down.shape, F32),
            pltpu.VMEM(block_mix.shape, F32),
            pltpu.VMEM(twist_hi.shape, F32),
            pltpu.VMEM(twist_lo.shape, F32),
            pltpu.VMEM((1, width), F32),
            pltpu.VMEM((NB, rows, 2 * FB), F32),
            pltpu.VMEM((NB, drows, DB), F32),
            pltpu.VMEM((2, count // 2, rows, 2 * FB), F32),
            pltpu.VMEM((2, count // 2, drows, DB), F32),
            pltpu.VMEM((DB, 2 * FB), F32),
            pltpu.VMEM((FB, DB), F32),
            pltpu.VMEM((DB, FB), F32),
            pltpu.VMEM((3 * DB, 2 * FB), BF16),
            pltpu.VMEM((DB, 6 * FB), BF16),
            pltpu.VMEM((FB, 3 * DB), BF16),
            pltpu.VMEM((2, count // 2, rows, 2 * FB), F32),
            pltpu.VMEM((2, count // 2, drows, DB), F32),
            pltpu.VMEM((reps, count // 2, rows, 2 * FB), F32),
            pltpu.VMEM((reps, count // 2, drows, DB), F32),
            pltpu.VMEM((count // 2, rows, 2 * FB), F32),
            pltpu.VMEM((count // 2, drows, DB), F32),
            pltpu.VMEM((reps, BLK + SMALL, DB), F32),
            pltpu.VMEM((BLK + SMALL, DB), F32),
            pltpu.VMEM((NB, part, DB), F32),
            pltpu.VMEM((part + SMALL, DB), F32),
            pltpu.VMEM((NB, NB, BLK), F32),
            pltpu.VMEM((NB, NB, BLK), F32),
            pltpu.VMEM((NB, BLK), F32),
        ]
        + [dma((many,))] * 31,
        compiler_params=pltpu.CompilerParams(
            collective_id=0, has_side_effects=True, vmem_limit_bytes=VMEM_LIMIT
        ),
        name="butterfly_block",
    )(inputs[0], cotangent[0], gate_up, down, block_mix, twist_hi, twist_lo, gain.reshape(1, width))
    outs = pl.pallas_call(
        lay_out,
        out_shape=tuple(
            jax.ShapeDtypeStruct(shape, F32)
            for shape in (
                (tokens, width), gate_up.shape, down.shape, block_mix.shape,
                twist_hi.shape, twist_lo.shape, (1, width),
            )
        ),
        in_specs=[hbm, vmem, vmem, vmem],
        out_specs=(hbm,) + (vmem,) * 6,
        scratch_shapes=[dma((PIECES,))],
        compiler_params=pltpu.CompilerParams(vmem_limit_bytes=VMEM_LIMIT),
        name="lay_out",
    )(out_x, out_gu, out_dn, out_small)
    return (outs[0][None],) + tuple(outs[1:6]) + (outs[6].reshape(width),)


def solution(mesh):
    return jax.shard_map(
        per_device,
        mesh=mesh,
        in_specs=(
            P("dp", "seq", None),
            P("dp", "seq", None),
            P(),
            P(),
            P(),
            P(),
            P("seq", None, None, None),
            P("seq", None, None),
        ),
        out_specs=(
            P("dp", "seq", None),
            P("seq", None, None, None),
            P("seq", None, None),
            P(),
            P(),
            P(),
            P(),
        ),
        check_vma=False,
    )
```

```python
import functools
import math

import jax
import jax.numpy as jnp
from jax import lax
from jax.experimental import pallas as pl
from jax.experimental.pallas import tpu as pltpu
from jax.sharding import PartitionSpec as P

NB = 16
BLK = 128
DB = 128
FB = 256
EPS = 1e-05
SMALL = 16
PIECES = 4
VMEM_LIMIT = 60 * 1024 * 1024
F32 = jnp.float32
BF16 = jnp.bfloat16
NN = (((1,), (0,)), ((), ()))
NT = (((1,), (1,)), ((), ()))
TN = (((0,), (0,)), ((), ()))
ORDER = (8, 1, 9, 2, 10, 3, 11, 4, 12, 5, 13, 6, 14, 7, 15)


def xor(a, b, bits):
    total = a + b
    for bit in range(bits):
        total = total - 2 * (1 << bit) * ((a // (1 << bit)) % 2) * ((b // (1 << bit)) % 2)
    return total


def split(value):
    high = value.astype(BF16)
    return high, (value - high.astype(F32)).astype(BF16)


def dot(a, b, dims):
    return lax.dot_general(a, b, dims, preferred_element_type=F32)


def left(value, axis):
    high, low = split(value)
    return jnp.concatenate([high, low, high], axis=axis)


def right(value, axis):
    high, low = split(value)
    return jnp.concatenate([high, high, low], axis=axis)


def row_sums(value):
    high, low = split(value)
    ones = jnp.ones((8, 2 * value.shape[1]), BF16)
    return dot(ones, jnp.concatenate([high, low], axis=1), NT)[0:1]


def as_columns(row):
    return jnp.broadcast_to(row, (DB, row.shape[1])).T


def arrived(ref, sem):
    pltpu.make_async_copy(ref, ref, sem).wait()


def kernel(
    dps, count, factor,
    x_hbm, g_hbm, gu_hbm, dn_hbm, bm_hbm, th_hbm, tl_hbm, gain_hbm,
    out_x, res_gu, res_dn, out_small,
    out_gu, out_dn, xb, gb, mixed, first, resid, scb, wsc, gseq,
    gu_ref, dn_ref, bm_ref, th_ref, tl_ref, gain_ref,
    gu_blk, dn_blk, gu_in, dn_in, gu_f32, dn_f32, dn_t, gu_k, gu_n, dn_n,
    gu_part, dn_part, gu_rep, dn_rep, gu_out, dn_out, sm_rep, sm_tot, bm_in, pack,
    ss_buf, in_buf, rows_ref,
    x_s, x_r, g_s, g_r, gu_s, gu_r, dn_s, dn_r, ss_s, ss_r, in_s, in_r,
    o_s, o_r, gr_s, gr_r, dr_s, dr_r, go_s, go_r, do_s, do_r, sr_s, sr_r,
    bm_s, bm_r, pk_s, pk_r, wx_s, wx_r, p_r,
):
    groups = count // NB
    bits = count.bit_length() - 1
    reps = dps * groups
    rows, drows = DB // count, FB // count
    me = lax.axis_index("seq")
    dp = lax.axis_index("dp")
    rank = me % 2 + me // (2 * groups) * 2
    group = me // 2 % groups
    rep = dp * groups + group
    half = dp % 2
    pair = dp + 1 - 2 * half
    odd = (me + half) % 2

    def seq_of(rk, grp):
        return rk % 2 + grp * 2 + rk // 2 * 2 * groups

    def peer(k):
        return seq_of(xor(rank, k, 4), group)

    def send(src, dst, ssem, rsem, to_dp, to_seq):
        copy = pltpu.make_async_remote_copy(
            src_ref=src, dst_ref=dst, send_sem=ssem, recv_sem=rsem,
            device_id=(to_dp, to_seq), device_id_type=pl.DeviceIdType.MESH,
        )
        copy.start()
        return copy

    def cols(ref, rk):
        return ref.at[:, pl.ds(pl.multiple_of(rk * DB, DB), DB)]

    replicas = []
    for step in range(1, reps):
        other = (rep + step) % reps
        replicas.append((step, other, other // groups, seq_of(rank, other % groups)))

    params = [
        pltpu.make_async_copy(src, dst, p_r.at[n])
        for n, (src, dst) in enumerate((
            (bm_hbm, bm_ref), (gu_hbm, gu_ref), (dn_hbm, dn_ref),
            (th_hbm, th_ref), (tl_hbm, tl_ref), (gain_hbm, gain_ref),
        ))
    ]
    local = [
        pltpu.make_async_copy(cols(x_hbm, rank), xb.at[0], x_r.at[0]),
        pltpu.make_async_copy(cols(g_hbm, rank), gb.at[0], g_r.at[0]),
    ]
    for copy in params + local:
        copy.start()

    barrier = pltpu.get_barrier_semaphore()
    met = 0
    for k in range(1, count):
        pl.semaphore_signal(
            barrier, inc=1, device_id=(dp, xor(me, k, bits)), device_id_type=pl.DeviceIdType.MESH
        )
        met += 1
    for step in range(1, dps):
        for grp in range(groups):
            pl.semaphore_signal(
                barrier, inc=1, device_id=((dp + step) % dps, seq_of(rank, grp)),
                device_id_type=pl.DeviceIdType.MESH,
            )
            met += 1
    pl.semaphore_wait(barrier, met)

    sent = []
    for k in ORDER:
        sent.append(send(cols(x_hbm, xor(rank, k, 4)), xb.at[k], x_s.at[k], x_r.at[k], dp, peer(k)))

    for copy in params:
        copy.wait()

    def weight_copies(k):
        to = xor(me, k, bits)
        block = to % 2 + to // (2 * groups) * 2
        slot = me // 2
        return [
            pltpu.make_async_remote_copy(
                src_ref=src.at[block], dst_ref=dst.at[half, slot], send_sem=ssem.at[k],
                recv_sem=rsem.at[k], device_id=(dp, to), device_id_type=pl.DeviceIdType.MESH,
            )
            for src, dst, ssem, rsem in ((gu_blk, gu_in, gu_s, gu_r), (dn_blk, dn_in, dn_s, dn_r))
        ]

    @pl.when(odd == 0)
    def _():
        for n in range(NB):
            for j in range(2):
                gu_blk[n, :, j * FB : (j + 1) * FB] = gu_ref[:, j, n, :]
            dn_blk[n] = dn_ref[:, n, :]
        pltpu.make_async_copy(gu_blk.at[rank], gu_in.at[half, me // 2], gu_r.at[0]).start()
        pltpu.make_async_copy(dn_blk.at[rank], dn_in.at[half, me // 2], dn_r.at[0]).start()
        for j in range(1, count):
            for copy in weight_copies(ORDER[j - 1] if count == NB else j):
                copy.start()

    mix_left = left(bm_ref[...], 1)
    back_left = left(bm_ref[...].T, 1)

    def mix(k, _):
        arrived(xb.at[k], x_r.at[k])
        mixed[k] = dot(mix_left, right(xb[k], 0), NN)
        return 0

    lax.fori_loop(0, NB // 2, mix, 0)
    for k in ORDER:
        sent.append(send(cols(g_hbm, xor(rank, k, 4)), gb.at[k], g_s.at[k], g_r.at[k], dp, peer(k)))
    lax.fori_loop(NB // 2, NB, mix, 0)

    lanes = pl.ds(pl.multiple_of(rank * DB, DB), DB)
    side_hi, side_lo = rank // 8, rank % 2

    def coefficients(ref, side):
        out = []
        for j in range(2):
            pair = ref[side + j - 2 * side * j, :, lanes]
            out.append((pair[0:1], pair[1:2]))
        return out

    hi = coefficients(th_ref, side_hi)
    lo = coefficients(tl_ref, side_lo)
    gain = gain_ref[:, lanes]

    def forward(i, _):
        ks = [2 * i, 2 * i + 1, 2 * i + 8, 2 * i + 9]
        mx = [mixed[k] for k in ks]
        fs = []
        for n in range(4):
            c = hi[n // 2]
            fs.append(c[0] * mx[n] + c[1] * mx[(n + 2) % 4])
            first[ks[n]] = fs[n]
        for n in range(4):
            c = lo[n % 2]
            r = xb[ks[n]] + (c[0] * fs[n] + c[1] * fs[n + 1 - 2 * (n % 2)])
            resid[ks[n]] = r
            ss_buf[0, pl.ds(xor(rank, ks[n], 4), 1), :] = row_sums(r * r)
        return 0

    lax.fori_loop(0, 4, forward, 0)
    for k in ORDER:
        sent.append(send(ss_buf.at[0], ss_buf.at[k], ss_s.at[k], ss_r.at[k], dp, peer(k)))

    for j in range(count // 2):
        k = 2 * j + odd
        owner = xor(me, k, bits)
        arrived(gu_in.at[half, owner // 2], gu_r.at[k])
        arrived(dn_in.at[half, owner // 2], dn_r.at[k])
    sent.append(send(gu_in.at[half], gu_in.at[half], wx_s.at[0], wx_r.at[0], pair, me))
    sent.append(send(dn_in.at[half], dn_in.at[half], wx_s.at[1], wx_r.at[1], pair, me))
    arrived(gu_in.at[1 - half], wx_r.at[0])
    arrived(dn_in.at[1 - half], wx_r.at[1])
    for s in range(count):
        gu_f32[s * rows : (s + 1) * rows, :] = gu_in[s % 2, s // 2]
        dn_f32[s * drows : (s + 1) * drows, :] = dn_in[s % 2, s // 2]
    gu_k[...] = right(gu_f32[...], 0)
    gu_n[...] = right(gu_f32[...], 1)
    dn_n[...] = right(dn_f32[...], 1)
    gu_f32[...] = jnp.zeros((DB, 2 * FB), F32)
    dn_t[...] = jnp.zeros((DB, FB), F32)

    for k in range(1, NB):
        arrived(ss_buf.at[k], ss_r.at[k])
    total = ss_buf[0]
    for k in range(1, NB):
        total = total + ss_buf[k]
    width = NB * DB
    rows_ref[...] = lax.rsqrt(total * (1.0 / width) + EPS)

    def mlp(i, gain_sum):
        scales, resids, cots = [], [], []
        for j in range(2):
            k = 2 * i + j
            arrived(gb.at[k], g_r.at[k])
            sc = as_columns(rows_ref[pl.ds(xor(rank, k, 4), 1), :])
            scb[k] = sc
            scales.append(sc)
            resids.append(resid[k])
            cots.append(gb[k])
        scale = jnp.concatenate(scales, axis=0)
        res = jnp.concatenate(resids, axis=0)
        cot = jnp.concatenate(cots, axis=0)
        unit = res * scale
        nh, nl = split(unit * gain)
        gh, gl = split(cot)
        gu = dot(jnp.concatenate([nh, nl, nh], axis=1), gu_k[...], NN)
        gate, up = gu[:, :FB], gu[:, FB:]
        sig = 1.0 / (1.0 + jnp.exp(-gate))
        act = gate * sig
        grad_hidden = dot(jnp.concatenate([gh, gl, gh], axis=1), dn_n[...], NT)
        hidden = right(act * up, 0)
        grad_gate = grad_hidden * up * sig * (1.0 + gate * (1.0 - sig))
        both_h, both_l = split(jnp.concatenate([grad_gate, grad_hidden * act], axis=1))
        grad_normed = dot(jnp.concatenate([both_h, both_l, both_h], axis=1), gu_n[...], NT)
        gu_f32[...] += dot(
            jnp.concatenate([nh, nl, nh], axis=0),
            jnp.concatenate([both_h, both_h, both_l], axis=0), TN,
        )
        dn_t[...] += dot(jnp.concatenate([gh, gl, gh], axis=0), hidden, TN)
        weighted = grad_normed * gain
        prod = weighted * res
        ws = weighted * scale
        for j in range(2):
            k = 2 * i + j
            wsc[k] = ws[j * BLK : (j + 1) * BLK]
            in_buf[0, pl.ds(xor(rank, k, 4), 1), :] = row_sums(prod[j * BLK : (j + 1) * BLK])
        return gain_sum + jnp.sum(grad_normed * unit, axis=0, keepdims=True)

    gain_sum = lax.fori_loop(0, NB // 2, mlp, jnp.zeros((1, DB), F32))

    for k in ORDER:
        sent.append(send(in_buf.at[0], in_buf.at[k], in_s.at[k], in_r.at[k], dp, peer(k)))
    dn_f32[...] = dn_t[...].T
    for s in range(count):
        gu_part[s % 2, s // 2] = gu_f32[s * rows : (s + 1) * rows, :]
        dn_part[s % 2, s // 2] = dn_f32[s * drows : (s + 1) * drows, :]
    for step, other, to_dp, to_seq in replicas:
        theirs = to_dp % 2
        sent.append(send(gu_part.at[theirs], gu_rep.at[rep], gr_s.at[step], gr_r.at[step], to_dp, to_seq))
        sent.append(send(dn_part.at[theirs], dn_rep.at[rep], dr_s.at[step], dr_r.at[step], to_dp, to_seq))
    gu_rep[rep] = gu_part[half]
    dn_rep[rep] = dn_part[half]

    for k in range(1, NB):
        arrived(in_buf.at[k], in_r.at[k])
    total = in_buf[0]
    for k in range(1, NB):
        total = total + in_buf[k]
    rows_ref[...] = total * (1.0 / width)

    sm_rep[rep] = jnp.zeros((BLK + SMALL, DB), F32)

    def backward(i, carry):
        q = 3 - i
        ks = [2 * q, 2 * q + 1, 2 * q + 8, 2 * q + 9]
        t_hi, t_lo = list(carry[:4]), list(carry[4:])
        gr = []
        for k in ks:
            inner = as_columns(rows_ref[pl.ds(xor(rank, k, 4), 1), :])
            sc = scb[k]
            gr.append(gb[k] + wsc[k] - resid[k] * sc * sc * sc * inner)
        fs = [first[k] for k in ks]
        mx = [mixed[k] for k in ks]
        gf = []
        for n in range(4):
            j, m = n % 2, n + 1 - 2 * (n % 2)
            gf.append(lo[j][0] * gr[n] + lo[1 - j][1] * gr[m])
            t_lo[2 * j] += jnp.sum(gr[n] * fs[n], axis=0, keepdims=True)
            t_lo[2 * j + 1] += jnp.sum(gr[n] * fs[m], axis=0, keepdims=True)
        for n in range(4):
            j, m = n // 2, (n + 2) % 4
            gm = hi[j][0] * gf[n] + hi[1 - j][1] * gf[m]
            t_hi[2 * j] += jnp.sum(gf[n] * mx[n], axis=0, keepdims=True)
            t_hi[2 * j + 1] += jnp.sum(gf[n] * mx[m], axis=0, keepdims=True)
            mh, ml = split(gm)
            gseq[ks[n]] = dot(back_left, jnp.concatenate([mh, mh, ml], axis=0), NN) + gr[n]
            k = ks[n]

            @pl.when(k != 0)
            def _():
                send(gseq.at[k], cols(out_x, rank), o_s.at[k], o_r.at[k], dp, peer(k))

            sm_rep[rep, :BLK, :] += dot(jnp.concatenate([mh, ml, mh], axis=1), right(xb[k], 1), NT)
        return tuple(t_hi + t_lo)

    zero = jnp.zeros((1, DB), F32)
    terms = lax.fori_loop(0, 2, backward, (zero,) * 8)

    for step, other, to_dp, to_seq in replicas:
        source = (rep + reps - step) % reps
        arrived(gu_rep.at[source], gr_r.at[step])
        arrived(dn_rep.at[source], dr_r.at[step])
    gu_sum, dn_sum = gu_rep[0], dn_rep[0]
    for other in range(1, reps):
        gu_sum = gu_sum + gu_rep[other]
        dn_sum = dn_sum + dn_rep[other]
    gu_out[...] = gu_sum * factor
    dn_out[...] = dn_sum * factor

    def grad_copies(k):
        to = peer(k)
        return [
            pltpu.make_async_remote_copy(
                src_ref=src.at[to // 2], dst_ref=dst.at[rank], send_sem=ssem.at[k],
                recv_sem=rsem.at[k], device_id=(dp, to), device_id_type=pl.DeviceIdType.MESH,
            )
            for src, dst, ssem, rsem in ((gu_out, out_gu, go_s, go_r), (dn_out, out_dn, do_s, do_r))
        ]

    swap = [
        pltpu.make_async_remote_copy(
            src_ref=ref, dst_ref=ref, send_sem=wx_s.at[n], recv_sem=wx_r.at[n],
            device_id=(pair, me), device_id_type=pl.DeviceIdType.MESH,
        )
        for n, ref in ((2, out_gu), (3, out_dn))
    ]

    @pl.when(odd == 0)
    def _():
        pltpu.make_async_copy(gu_out.at[me // 2], out_gu.at[rank], go_r.at[0]).start()
        pltpu.make_async_copy(dn_out.at[me // 2], out_dn.at[rank], do_r.at[0]).start()

    for j in reversed(range(NB // 2)):
        k = 2 * j + odd

        @pl.when(k != 0)
        def _():
            for copy in grad_copies(k):
                copy.start()

    terms = lax.fori_loop(2, 4, backward, terms)
    own_x = pltpu.make_async_copy(gseq.at[0], cols(out_x, rank), o_r.at[0])
    own_x.start()
    for j in range(2):
        for c in range(2):
            place = 2 * (side_hi + j - 2 * side_hi * j) + c
            sm_rep[rep, pl.ds(BLK + place, 1), :] = terms[2 * j + c]
            place = 2 * (side_lo + j - 2 * side_lo * j) + c
            sm_rep[rep, pl.ds(BLK + 4 + place, 1), :] = terms[4 + 2 * j + c]
    sm_rep[rep, BLK + 8 : BLK + 9, :] = gain_sum
    for step, other, to_dp, to_seq in replicas:
        sent.append(send(sm_rep.at[rep], sm_rep.at[rep], sr_s.at[step], sr_r.at[step], to_dp, to_seq))

    @pl.when(odd == 0)
    def _():
        for k in range(NB):
            source = xor(rank, k, 4)
            arrived(out_gu.at[source], go_r.at[k])
            arrived(out_dn.at[source], do_r.at[k])
        for copy in swap:
            copy.start()

    for step, other, to_dp, to_seq in replicas:
        source = (rep + reps - step) % reps
        arrived(sm_rep.at[source], sr_r.at[step])
    sm_sum = sm_rep[0]
    for other in range(1, reps):
        sm_sum = sm_sum + sm_rep[other]
    sm_tot[...] = sm_sum * factor
    part = BLK // NB

    def part_of(rk):
        return sm_tot.at[pl.ds(pl.multiple_of(rk * part, part), part), :]

    for k in ORDER:
        sent.append(send(part_of(xor(rank, k, 4)), bm_in.at[k], bm_s.at[k], bm_r.at[k], dp, peer(k)))
    bm_sum = sm_tot[pl.ds(pl.multiple_of(rank * part, part), part), :]
    for k in range(1, NB):
        arrived(bm_in.at[k], bm_r.at[k])
        bm_sum = bm_sum + bm_in[k]
    pack[0:part, :] = bm_sum
    pack[part : part + SMALL, :] = sm_tot[BLK : BLK + SMALL, :]
    for k in ORDER:
        sent.append(send(pack, out_small.at[rank], pk_s.at[k], pk_r.at[k], dp, peer(k)))
    own = [own_x, pltpu.make_async_copy(pack, out_small.at[rank], pk_r.at[0])]
    own[1].start()

    for copy in own:
        copy.wait()
    for k in range(1, NB):
        source = xor(rank, k, 4)
        arrived(cols(out_x, source), o_r.at[k])
        arrived(out_small.at[source], pk_r.at[k])
        arrived(gseq.at[k], o_s.at[k])
    for copy in sent:
        copy.wait_send()

    @pl.when(odd == 0)
    def _():
        for copy in swap:
            copy.wait_send()
        for k in range(1, count):
            for copy in weight_copies(k):
                copy.wait_send()

    @pl.when(odd == 1)
    def _():
        for copy in swap:
            copy.wait_recv()

    results = [
        pltpu.make_async_copy(out_gu, res_gu, p_r.at[0]),
        pltpu.make_async_copy(out_dn, res_dn, p_r.at[1]),
    ]
    for copy in results:
        copy.start()

    for j in range(NB // 2):
        k = 2 * j + odd

        @pl.when(k != 0)
        def _():
            for copy in grad_copies(k):
                copy.wait_send()

    for copy in results:
        copy.wait()


def lay_out(x_in, gu_in, dn_in, small, x_out, gu_out, dn_out, bm_out, th_out, tl_out, gain_out, field, in_sem, out_sem):
    rows = x_in.shape[0] // PIECES
    spans = [slice(n * rows, (n + 1) * rows) for n in range(PIECES)]
    loads = [
        pltpu.make_async_copy(x_in.at[at], field.at[at], in_sem.at[n]) for n, at in enumerate(spans)
    ]
    stores = [
        pltpu.make_async_copy(field.at[at], x_out.at[at], out_sem.at[n]) for n, at in enumerate(spans)
    ]
    for copy in loads:
        copy.start()
    for load, store in zip(loads, stores):
        load.wait()
        store.start()
    part = BLK // NB
    for n in range(NB):
        lanes = slice(n * DB, (n + 1) * DB)
        for j in range(2):
            gu_out[:, j, n, :] = gu_in[n, :, j * FB : (j + 1) * FB]
            th_out[j, :, lanes] = small[n, part + 2 * j : part + 2 * j + 2, :]
            tl_out[j, :, lanes] = small[n, part + 4 + 2 * j : part + 6 + 2 * j, :]
        dn_out[:, n, :] = dn_in[n]
        bm_out[n * part : (n + 1) * part, :] = small[n, 0:part, :]
        gain_out[:, lanes] = small[n, part + 8 : part + 9, :]
    for copy in stores:
        copy.wait()


def per_device(inputs, cotangent, block_mix, twist_hi, twist_lo, gain, gate_up, down):
    tokens, width = inputs.shape[1:]
    count = lax.axis_size("seq")
    dps = lax.axis_size("dp")
    groups = count // NB
    reps = dps * groups
    rows, drows = gate_up.shape[0], down.shape[0]
    factor = 1.0 / math.sqrt(dps * count * tokens)
    vmem = pl.BlockSpec(memory_space=pltpu.VMEM)
    hbm = pl.BlockSpec(memory_space=pl.ANY)
    dma = pltpu.SemaphoreType.DMA
    part = BLK // NB
    field = pltpu.VMEM((NB, tokens, DB), F32)
    many = max(count, reps)
    out_x, out_gu, out_dn, out_small = pl.pallas_call(
        functools.partial(kernel, dps, count, factor),
        out_shape=(
            jax.ShapeDtypeStruct((tokens, width), F32),
            jax.ShapeDtypeStruct((NB, rows, 2 * FB), F32),
            jax.ShapeDtypeStruct((NB, drows, DB), F32),
            jax.ShapeDtypeStruct((NB, part + SMALL, DB), F32),
        ),
        in_specs=[pl.BlockSpec(memory_space=pltpu.HBM)] * 8,
        out_specs=(hbm, hbm, hbm, hbm),
        scratch_shapes=[
            pltpu.VMEM((NB, rows, 2 * FB), F32),
            pltpu.VMEM((NB, drows, DB), F32),
        ]
        + [field] * 8
        + [
            pltpu.VMEM(gate_up.shape, F32),
            pltpu.VMEM(down.shape, F32),
            pltpu.VMEM(block_mix.shape, F32),
            pltpu.VMEM(twist_hi.shape, F32),
            pltpu.VMEM(twist_lo.shape, F32),
            pltpu.VMEM((1, width), F32),
            pltpu.VMEM((NB, rows, 2 * FB), F32),
            pltpu.VMEM((NB, drows, DB), F32),
            pltpu.VMEM((2, count // 2, rows, 2 * FB), F32),
            pltpu.VMEM((2, count // 2, drows, DB), F32),
            pltpu.VMEM((DB, 2 * FB), F32),
            pltpu.VMEM((FB, DB), F32),
            pltpu.VMEM((DB, FB), F32),
            pltpu.VMEM((3 * DB, 2 * FB), BF16),
            pltpu.VMEM((DB, 6 * FB), BF16),
            pltpu.VMEM((FB, 3 * DB), BF16),
            pltpu.VMEM((2, count // 2, rows, 2 * FB), F32),
            pltpu.VMEM((2, count // 2, drows, DB), F32),
            pltpu.VMEM((reps, count // 2, rows, 2 * FB), F32),
            pltpu.VMEM((reps, count // 2, drows, DB), F32),
            pltpu.VMEM((count // 2, rows, 2 * FB), F32),
            pltpu.VMEM((count // 2, drows, DB), F32),
            pltpu.VMEM((reps, BLK + SMALL, DB), F32),
            pltpu.VMEM((BLK + SMALL, DB), F32),
            pltpu.VMEM((NB, part, DB), F32),
            pltpu.VMEM((part + SMALL, DB), F32),
            pltpu.VMEM((NB, NB, BLK), F32),
            pltpu.VMEM((NB, NB, BLK), F32),
            pltpu.VMEM((NB, BLK), F32),
        ]
        + [dma((many,))] * 31,
        compiler_params=pltpu.CompilerParams(
            collective_id=0, has_side_effects=True, vmem_limit_bytes=VMEM_LIMIT
        ),
        name="butterfly_block",
    )(inputs[0], cotangent[0], gate_up, down, block_mix, twist_hi, twist_lo, gain.reshape(1, width))
    outs = pl.pallas_call(
        lay_out,
        out_shape=tuple(
            jax.ShapeDtypeStruct(shape, F32)
            for shape in (
                (tokens, width), gate_up.shape, down.shape, block_mix.shape,
                twist_hi.shape, twist_lo.shape, (1, width),
            )
        ),
        in_specs=[hbm, vmem, vmem, vmem],
        out_specs=(hbm,) + (vmem,) * 6,
        scratch_shapes=[pltpu.VMEM((tokens, width), F32), dma((PIECES,)), dma((PIECES,))],
        compiler_params=pltpu.CompilerParams(vmem_limit_bytes=VMEM_LIMIT),
        name="lay_out",
    )(out_x, out_gu, out_dn, out_small)
    return (outs[0][None],) + tuple(outs[1:6]) + (outs[6].reshape(width),)


def solution(mesh):
    return jax.shard_map(
        per_device,
        mesh=mesh,
        in_specs=(
            P("dp", "seq", None),
            P("dp", "seq", None),
            P(),
            P(),
            P(),
            P(),
            P("seq", None, None, None),
            P("seq", None, None),
        ),
        out_specs=(
            P("dp", "seq", None),
            P("seq", None, None, None),
            P("seq", None, None),
            P(),
            P(),
            P(),
            P(),
        ),
        check_vma=False,
    )
```
